128 devices in a mesh: node: 8 (over z, core), local: 16 (over x, y).
Axes of the slice: x: 4, y: 4, z: 4, core: 2. Of those that a mesh axis runs over, the one named last changes fastest.
Arguments:
- patches: bfloat16 [1024, 1408], P('node'), may hold values from -6 to 6
- norm_gain: float32 [1408], replicated, may hold values from 0.25 to 1.75
- vit_up: bfloat16 [1408, 5632], P(None, 'local'), may hold values from -0.15625 to 0.15625
- vit_down: bfloat16 [5632, 1408], P('local'), may hold values from -0.078125 to 0.078125
- adapter: bfloat16 [1408, 5120], P('local'), may hold values from -0.15625 to 0.15625
- text_rows: bfloat16 [15360, 5120], P(('node', 'local')), may hold values from -6 to 6
- router: bfloat16 [5120, 8], replicated, may hold values from -0.15625 to 0.15625
- expert_ids: int32 [16384, 1], P(('node', 'local')), may hold values from 0 to 7
- w_gate: bfloat16 [8, 5120, 4096], P('node', None, 'local'), may hold values from -0.15625 to 0.15625
- w_up: bfloat16 [8, 5120, 4096], P('node', None, 'local'), may hold values from -0.15625 to 0.15625
- w_down: bfloat16 [8, 4096, 5120], P('node', 'local'), may hold values from -0.25 to 0.25
Outputs:
- expert_out: bfloat16 [8, 1792, 5120], P('node', 'local')
The draws below stay inside these ranges and needn't reach their ends.
All inputs are finite; a program needn't handle non-finite values.
Results may differ from the reference program's by a relative error of at most 0.029.
Values may be sent and summed in bfloat16 or wider, within the bound.
A program may use at most 128 MiB of HBM per device.

```python
import jax
import jax.numpy as jnp
from jax import lax

D = 5120
VW = 1408
VFF = 5632
FE = 4096
ROWS_DEV = 128
VIS_DEV = 8
TXT_DEV = 120
EXPERTS = 8
CAP = 14
SLOTS = 1792
VIS_ROWS = 1024
TXT_ROWS = 15360
ALL_ROWS = 16384
N_NODE = 8
N_LOCAL = 16
DEVICES = 128


def block_levels(rng, dims, split, least, high):
    level, own = 1.0, jax.random.fold_in(rng, 6)
    for dim, parts in split:
        draws = jnp.exp(jax.random.uniform(jax.random.fold_in(own, dim), (parts,), jnp.float32, least / len(split), high / len(split)))
        level = level * jnp.repeat(draws, dims[dim] // parts).reshape([-1 if axis == dim else 1 for axis in range(len(dims))])
    return level


def different_ones(key, rows, number_of, top, lift):
    ranking = jax.random.permutation(jax.random.fold_in(key, 1), number_of)
    pull = ranking
    for power in range(3):
        pull = pull * pull // number_of
    pull = pull * lift // number_of
    tickets = jax.random.randint(jax.random.fold_in(key, 2), (rows, number_of), 0, 4096) + pull
    fixed_rows = jax.random.permutation(jax.random.fold_in(key, 3), rows)[jnp.arange(number_of) % rows]
    tickets = jnp.where(jnp.arange(rows)[:, None] == fixed_rows[None, :], 1 << 14, tickets)
    priority = tickets * number_of + jnp.arange(number_of)
    return lax.top_k(priority.astype(jnp.int32), top)[1].astype(jnp.int32)


def normal_values(key, shape, scale, most, pieces=(), kind=jnp.bfloat16):
    loudness = block_levels(key, shape, pieces, -0.22, 0.18) if pieces else 1.0
    result = jax.random.normal(key, shape, jnp.float32) * scale * loudness
    return jnp.minimum(jnp.maximum(result, -most), most).astype(kind)


def setup_inputs(seed: int = 0) -> dict:
    streams_of = jax.random.split(jax.random.key(seed), 12)
    patches = normal_values(streams_of[0], (VIS_ROWS, VW), 1.0, 6.0, ((0, 8),))
    norm_gain = jnp.clip(1.0 + 0.15 * jax.random.normal(streams_of[1], (VW,), jnp.float32), 0.25, 1.75)
    vit_up = normal_values(streams_of[2], (VW, VFF), VW ** -0.5, 0.15625, ((1, 16),))
    vit_down = normal_values(streams_of[3], (VFF, VW), VFF ** -0.5, 0.078125, ((0, 16),))
    adapter = normal_values(streams_of[4], (VW, D), VW ** -0.5, 0.15625, ((0, 16),))
    text_rows = normal_values(streams_of[5], (TXT_ROWS, D), 1.0, 6.0, ((0, 128),))
    router = normal_values(streams_of[6], (D, EXPERTS), (D // 4) ** -0.5, 0.15625)
    expert_ids = different_ones(streams_of[7], ALL_ROWS, EXPERTS, 1, 2048)
    w_gate = normal_values(streams_of[8], (EXPERTS, D, FE), (D // 4) ** -0.5, 0.15625, ((0, 8), (2, 16)))
    w_up = normal_values(streams_of[9], (EXPERTS, D, FE), (D // 4) ** -0.5, 0.15625, ((0, 8), (2, 16)))
    w_down = normal_values(streams_of[10], (EXPERTS, FE, D), (FE // 8) ** -0.5, 0.25, ((0, 8), (1, 16)))
    return {"patches": patches, "norm_gain": norm_gain, "vit_up": vit_up, "vit_down": vit_down, "adapter": adapter, "text_rows": text_rows, "router": router, "expert_ids": expert_ids, "w_gate": w_gate, "w_up": w_up, "w_down": w_down}


def layer_norm(rows, gain):
    values = rows.astype(jnp.float32)
    center = lax.optimization_barrier(jnp.mean(values, axis=-1, keepdims=True))
    spread = lax.optimization_barrier(jnp.mean((values - center) ** 2, axis=-1, keepdims=True))
    return (values - center) * lax.rsqrt(spread + 1e-05) * gain

def reference(patches, norm_gain, vit_up, vit_down, adapter, text_rows, router, expert_ids, w_gate, w_up, w_down):
    normed = layer_norm(patches, norm_gain).astype(jnp.bfloat16)
    inner = jax.nn.gelu(jnp.dot(normed, vit_up, preferred_element_type=jnp.float32), approximate=True).astype(jnp.bfloat16)
    vision = (patches.astype(jnp.float32) + jnp.dot(inner, vit_down, preferred_element_type=jnp.float32)).astype(jnp.bfloat16)
    block = VW // N_LOCAL
    embed = jnp.zeros((VIS_ROWS, D), jnp.float32)
    for index in range(N_LOCAL):
        term = jnp.dot(vision[:, index * block:(index + 1) * block], adapter[index * block:(index + 1) * block], preferred_element_type=jnp.float32)
        embed = embed + term.astype(jnp.bfloat16).astype(jnp.float32)
    embed = embed.astype(jnp.bfloat16)
    seq = jnp.concatenate([text_rows.reshape(DEVICES, TXT_DEV, D), embed.reshape(DEVICES, VIS_DEV, D)], axis=1)
    logits = jnp.einsum('grd,de->gre', seq.astype(jnp.float32), router.astype(jnp.float32))
    chosen = expert_ids.reshape(DEVICES, ROWS_DEV)
    table = (chosen[:, :, None] == jnp.arange(EXPERTS, dtype=jnp.int32)[None, None, :]).astype(jnp.int32)
    score = jax.nn.sigmoid(lax.optimization_barrier(jnp.sum(logits * table.astype(jnp.float32), axis=-1)))
    scaled = (seq.astype(jnp.float32) * score[:, :, None]).astype(jnp.bfloat16)
    rank = lax.optimization_barrier(jnp.sum((jnp.cumsum(table, axis=1) - 1) * table, axis=-1))
    slot = chosen * CAP + rank
    place = ((slot[:, None, :] == jnp.arange(EXPERTS * CAP, dtype=jnp.int32)[None, :, None]) & (rank < CAP)[:, None, :]).astype(jnp.float32)
    sent = jnp.einsum('gkr,grd->gkd', place, scaled.astype(jnp.float32)).astype(jnp.bfloat16)
    sent = sent.reshape(N_NODE, N_LOCAL, EXPERTS, CAP, D)
    width = FE // N_LOCAL
    results = []
    for expert in range(EXPERTS):
        rows = jnp.transpose(sent[:, :, expert], (1, 0, 2, 3)).reshape(SLOTS, D)
        total = jnp.zeros((SLOTS, D), jnp.float32)
        for index in range(N_LOCAL):
            low = index * width
            gate = jnp.dot(rows, w_gate[expert, :, low:low + width], preferred_element_type=jnp.float32)
            upper = jnp.dot(rows, w_up[expert, :, low:low + width], preferred_element_type=jnp.float32)
            hidden = (jax.nn.silu(gate) * upper).astype(jnp.bfloat16)
            term = jnp.dot(hidden, w_down[expert, low:low + width], preferred_element_type=jnp.float32)
            total = total + term.astype(jnp.bfloat16).astype(jnp.float32)
        results.append(total.astype(jnp.bfloat16))
    return jnp.stack(results, axis=0)
```

```python
import jax
import jax.numpy as jnp
from jax import lax
from jax.experimental import pallas as pl
from jax.experimental.pallas import tpu as pltpu
from jax.sharding import PartitionSpec as P

MESH = pl.DeviceIdType.MESH
BF = jnp.bfloat16
F32 = jnp.float32
SIDE = 4
PAD = 16


def remote(src, dst, send_sem, recv_sem, device):
    return pltpu.make_async_remote_copy(
        src_ref=src,
        dst_ref=dst,
        send_sem=send_sem,
        recv_sem=recv_sem,
        device_id=device,
        device_id_type=MESH,
    )


def greet(devices):
    barrier = pltpu.get_barrier_semaphore()
    for device in devices:
        pl.semaphore_signal(barrier, inc=1, device_id=device, device_id_type=MESH)
    pl.semaphore_wait(barrier, len(devices))


def vision_kernel(
    n_local,
    capacity,
    patches_ref,
    gain_ref,
    up_ref,
    down_ref,
    adapter_ref,
    text_ref,
    router_ref,
    ids_ref,
    out_ref,
    part_send,
    part_recv,
    patch_blocks,
    embed_send,
    embed_recv,
    sems,
):
    node, local = lax.axis_index("node"), lax.axis_index("local")
    peers = [(node, lax.rem(local + k, n_local)) for k in range(1, n_local)]
    greet(peers)

    rows, width = patches_ref.shape
    block = width // n_local
    values = patches_ref[...].astype(F32)
    center = jnp.mean(values, axis=-1, keepdims=True)
    spread = jnp.mean((values - center) ** 2, axis=-1, keepdims=True)
    normed = ((values - center) * lax.rsqrt(spread + 1e-05) * gain_ref[...]).astype(BF)
    inner = jax.nn.gelu(
        jnp.dot(normed, up_ref[...], preferred_element_type=F32), approximate=True
    ).astype(BF)
    partial_sum = jnp.dot(inner, down_ref[...], preferred_element_type=F32)
    for index in range(n_local):
        low = index * block
        part_send[index, :, 0:block] = partial_sum[:, low : low + block].astype(BF)
        patch_blocks[index, :, 0:block] = values[:, low : low + block].astype(BF)

    first = []
    for k in range(1, n_local):
        copy = remote(
            part_send.at[peers[k - 1][1]],
            part_recv.at[k],
            sems.at[0, k],
            sems.at[1, k],
            peers[k - 1],
        )
        copy.start()
        first.append(copy)

    text_rows, model = text_ref.shape
    all_rows = ids_ref.shape[0]
    experts = router_ref.shape[1]
    chosen = ids_ref[...]
    table = (
        chosen == lax.broadcasted_iota(jnp.int32, (all_rows, experts), 1)
    ).astype(F32)
    earlier = (
        lax.broadcasted_iota(jnp.int32, (all_rows, all_rows), 0)
        > lax.broadcasted_iota(jnp.int32, (all_rows, all_rows), 1)
    ).astype(BF)
    counts = jnp.dot(earlier, table.astype(BF), preferred_element_type=F32)
    rank = jnp.sum(counts * table, axis=1, keepdims=True).astype(jnp.int32)
    slot = jnp.where(rank < capacity, chosen * PAD + rank, -1)
    place = jnp.transpose(
        (slot == lax.broadcasted_iota(jnp.int32, (all_rows, experts * PAD), 1)).astype(F32)
    ).astype(BF)
    logits = jnp.dot(text_ref[...], router_ref[...], preferred_element_type=F32)
    score = jax.nn.sigmoid(
        jnp.sum(logits * table[0:text_rows], axis=1, keepdims=True)
    )
    step = 512

    def place_text(index, carry):
        columns = pl.ds(pl.multiple_of(index * step, step), step)
        scaled = text_ref[:, columns].astype(F32) * score
        scaled = jnp.concatenate(
            [scaled, jnp.zeros((all_rows - text_rows, step), F32)], axis=0
        ).astype(BF)
        sent = jnp.dot(place, scaled, preferred_element_type=F32).astype(BF)
        for expert in range(experts):
            out_ref[expert, :, columns] = sent[expert * PAD : (expert + 1) * PAD]
        return carry

    lax.fori_loop(0, model // step, place_text, 0)

    total = part_send[local, :, 0:block].astype(F32)
    for k in range(1, n_local):
        first[k - 1].wait_recv()
        total = total + part_recv[k, :, 0:block].astype(F32)
    vision = (patch_blocks[local, :, 0:block].astype(F32) + total).astype(BF)

    half = model // 2
    own = rows // n_local
    wide = 640

    def embed_part(index, carry):
        low = pl.ds(pl.multiple_of(index * wide, 128), wide)
        high = pl.ds(pl.multiple_of(index * wide + half, 128), wide)
        left = jnp.dot(vision, adapter_ref[:, low], preferred_element_type=F32)
        right = jnp.dot(vision, adapter_ref[:, high], preferred_element_type=F32)
        for j in range(n_local):
            embed_send[j, :, low] = jnp.concatenate(
                [left[j * own : (j + 1) * own], right[j * own : (j + 1) * own]], axis=0
            ).astype(BF)
        return carry

    lax.fori_loop(0, half // wide, embed_part, 0)

    second = []
    for k in range(1, n_local):
        copy = remote(
            embed_send.at[peers[k - 1][1]],
            embed_recv.at[k],
            sems.at[2, k],
            sems.at[3, k],
            peers[k - 1],
        )
        copy.start()
        second.append(copy)
    for k in range(1, n_local):
        second[k - 1].wait_recv()

    embed = embed_send[local].astype(F32)
    for k in range(1, n_local):
        embed = embed + embed_recv[k].astype(F32)
    embed = embed.astype(BF).astype(F32)
    image = jnp.dot(
        embed[0:own].astype(BF), router_ref[0:half, :], preferred_element_type=F32
    ) + jnp.dot(
        embed[own : 2 * own].astype(BF), router_ref[half:model, :], preferred_element_type=F32
    )
    image_score = jax.nn.sigmoid(
        jnp.sum(image * table[text_rows:all_rows], axis=1, keepdims=True)
    )
    for part in range(2):
        for low in range(0, half, step):
            columns = slice(part * half + low, part * half + low + step)
            scaled = embed[part * own : (part + 1) * own, low : low + step] * image_score
            scaled = jnp.concatenate(
                [jnp.zeros((text_rows, step), F32), scaled], axis=0
            ).astype(BF)
            sent = jnp.dot(place, scaled, preferred_element_type=F32)
            for expert in range(experts):
                out_ref[expert, :, columns] = (
                    out_ref[expert, :, columns].astype(F32)
                    + sent[expert * PAD : (expert + 1) * PAD]
                ).astype(BF)
    for copy in first + second:
        copy.wait_send()


def expert_kernel(
    n_node,
    capacity,
    slots_ref,
    gate_hbm,
    up_hbm,
    down_hbm,
    out_ref,
    gate_ref,
    up_ref,
    down_ref,
    arrived,
    held,
    hidden,
    halves,
    fulls,
    load_sem,
    node_sem,
    gather_sem,
    reduce_sem,
):
    node, local = lax.axis_index("node"), lax.axis_index("local")
    core = lax.rem(node, 2)
    x, y = local // SIDE, lax.rem(local, SIDE)
    p1, p2 = jnp.where(core == 0, x, y), jnp.where(core == 0, y, x)
    s1, s2 = jnp.where(core == 0, SIDE, 1), jnp.where(core == 0, 1, SIDE)

    def shift(p, d):
        return lax.rem(p + d + SIDE, SIDE)

    def device(d1, d2):
        return (node, shift(p1, d1) * s1 + shift(p2, d2) * s2)

    def blk(d1, d2):
        return shift(p1, d1) * SIDE + shift(p2, d2)

    peers = [(lax.rem(node + k, n_node), local) for k in range(1, n_node)]
    rings = [(device(1, 0), device(-1, 0)), (device(0, 1), device(0, -1))]
    greet(peers + list(rings[0]) + list(rings[1]))

    loads = [
        pltpu.make_async_copy(gate_hbm.at[0], gate_ref, load_sem.at[0]),
        pltpu.make_async_copy(up_hbm.at[0], up_ref, load_sem.at[1]),
        pltpu.make_async_copy(down_hbm.at[0], down_ref, load_sem.at[2]),
    ]
    sends = []
    for k in range(1, n_node):
        copy = remote(
            slots_ref.at[peers[k - 1][0]],
            arrived.at[node],
            node_sem.at[0, k],
            node_sem.at[1, k],
            peers[k - 1],
        )
        copy.start()
        sends.append(copy)
    for load in loads:
        load.start()
    mine = pltpu.make_async_copy(slots_ref.at[node], arrived.at[node], load_sem.at[3])
    mine.start()
    for k in range(1, n_node):
        source = lax.rem(node + n_node - k, n_node)
        remote(
            arrived.at[source],
            arrived.at[source],
            node_sem.at[0, k],
            node_sem.at[1, k],
            peers[k - 1],
        ).wait_recv()
    mine.wait()

    rows, model = held.shape[1], held.shape[2]
    half = model // 2
    step = 512
    target = lax.broadcasted_iota(jnp.int32, (rows, n_node * PAD), 0)
    origin = lax.broadcasted_iota(jnp.int32, (rows, n_node * PAD), 1)
    pick = (target // capacity * PAD + lax.rem(target, capacity) == origin).astype(BF)
    home = blk(0, 0)

    def compact(index, carry):
        columns = pl.ds(pl.multiple_of(index * step, step), step)
        held[home, :, columns] = jnp.dot(
            pick,
            arrived[:, :, columns].reshape(n_node * PAD, step),
            preferred_element_type=F32,
        ).astype(BF)
        return carry

    lax.fori_loop(0, model // step, compact, 0)

    depth = 1280

    def ffn_in(block):
        def body(index, carry):
            gate, upper = carry
            deep = pl.ds(pl.multiple_of(index * depth, depth), depth)
            piece = held[block, :, deep]
            return (
                gate + jnp.dot(piece, gate_ref[deep, :], preferred_element_type=F32),
                upper + jnp.dot(piece, up_ref[deep, :], preferred_element_type=F32),
            )

        zero = jnp.zeros((rows, gate_ref.shape[1]), F32)
        gate, upper = lax.fori_loop(0, model // depth, body, (zero, zero))
        hidden[block] = (jax.nn.silu(gate) * upper).astype(BF)

    gather_waits = []

    def ring_send(op, ring, block, way):
        copy = remote(
            held.at[block],
            held.at[block],
            gather_sem.at[0, op, way],
            gather_sem.at[1, op, way],
            rings[ring][way],
        )
        copy.start()
        gather_waits.append(copy)

    def ring_recv(op, ring, block, way):
        remote(
            held.at[block],
            held.at[block],
            gather_sem.at[0, op, way],
            gather_sem.at[1, op, way],
            rings[ring][way],
        ).wait_recv()

    def half_copy(op, ring, block, way):
        part = held.at[block, :, pl.ds(way * half, half)]
        return remote(
            part,
            part,
            gather_sem.at[0, op, 2 + way],
            gather_sem.at[1, op, 2 + way],
            rings[ring][way],
        )

    def half_send(op, ring, block, way):
        copy = half_copy(op, ring, block, way)
        copy.start()
        gather_waits.append(copy)

    def half_recv(op, ring, block, way):
        half_copy(op, ring, block, way).wait_recv()

    for way in range(2):
        ring_send(0, 0, blk(0, 0), way)
    for way in range(2):
        ring_send(1, 1, blk(0, 0), way)
    loads[0].wait()
    loads[1].wait()
    ffn_in(blk(0, 0))
    sides = (-1, 1)
    for way in range(2):
        block = blk(sides[way], 0)
        ring_recv(0, 0, block, way)
        half_send(0, 0, block, way)
        for out in range(2):
            ring_send(2 + way, 1, block, out)
    for way in range(2):
        ffn_in(blk(sides[way], 0))
    for way in range(2):
        block = blk(0, sides[way])
        ring_recv(1, 1, block, way)
        half_send(1, 1, block, way)
    for way in range(2):
        half_recv(0, 0, blk(2, 0), way)
    for way in range(2):
        ring_send(4, 1, blk(2, 0), way)
    for way in range(2):
        ffn_in(blk(0, sides[way]))
    ffn_in(blk(2, 0))
    for way in range(2):
        half_recv(1, 1, blk(0, 2), way)
    ffn_in(blk(0, 2))
    for op, d1 in ((2, -1), (3, 1), (4, 2)):
        for way in range(2):
            block = blk(d1, sides[way])
            ring_recv(op, 1, block, way)
            half_send(op, 1, block, way)
        for way in range(2):
            ffn_in(blk(d1, sides[way]))
        if op > 2:
            before = {3: -1, 4: 1}[op]
            for way in range(2):
                half_recv(op - 1, 1, blk(before, 2), way)
            ffn_in(blk(before, 2))
    for way in range(2):
        half_recv(4, 1, blk(2, 2), way)
    ffn_in(blk(2, 2))
    loads[2].wait()

    reduce_waits = []
    order = (2, 1, -1, 0)

    def part_copy(op, ring, block, way):
        return remote(
            held.at[block, :, pl.ds(way * half, half)],
            halves.at[op, way],
            reduce_sem.at[0, op, way],
            reduce_sem.at[1, op, way],
            rings[ring][way],
        )

    def full_copy(op, ring, block, way):
        return remote(
            held.at[block],
            fulls.at[op, way],
            reduce_sem.at[0, op, 2 + way],
            reduce_sem.at[1, op, 2 + way],
            rings[ring][way],
        )

    def start(copy):
        copy.start()
        reduce_waits.append(copy)

    def ffn_out(block, dest, terms):
        for part in range(2):

            def body(index, carry):
                low = pl.multiple_of(index * step, step)
                columns = pl.ds(pl.multiple_of(low + part * half, step), step)
                value = jnp.dot(
                    hidden[block], down_ref[:, columns], preferred_element_type=F32
                )
                for term in terms:
                    if term[0] == "full":
                        value = value + fulls[term[1], term[2], :, columns].astype(F32)
                    elif term[2] == part:
                        value = value + halves[term[1], term[2], :, pl.ds(low, step)].astype(F32)
                dest[:, columns] = value.astype(BF)
                return carry

            lax.fori_loop(0, half // step, body, 0)

    def far(k):
        block = blk(order[k], 2)
        ffn_out(block, held.at[block], ())
        for way in range(2):
            start(part_copy(k, 1, block, way))

    def near(k):
        for way in range(2):
            block = blk(order[k], (1, -1)[way])
            part_copy(k, 1, block, way).wait_recv()
            ffn_out(block, held.at[block], (("half", k, way),))
            start(full_copy(k, 1, block, way))

    def own(k):
        block = blk(order[k], 0)
        for way in range(2):
            full_copy(k, 1, block, way).wait_recv()
        terms = [("full", k, 0), ("full", k, 1)]
        dest = held.at[block]
        if k in (1, 2):
            part_copy(4, 0, block, k - 1).wait_recv()
            terms.append(("half", 4, k - 1))
        if k == 3:
            for way in range(2):
                full_copy(4, 0, block, way).wait_recv()
                terms.append(("full", 4, way))
            dest = out_ref
        ffn_out(block, dest, terms)
        if k == 0:
            for way in range(2):
                start(part_copy(4, 0, block, way))
        elif k in (1, 2):
            start(full_copy(4, 0, block, k - 1))

    for k in range(4):
        far(k)
    for copy in gather_waits:
        copy.wait_send()
    near(0)
    near(1)
    own(0)
    near(2)
    own(1)
    near(3)
    own(2)
    own(3)
    for copy in sends + reduce_waits:
        copy.wait_send()


def on_device(n_node, n_local):
    def run(
        patches,
        norm_gain,
        vit_up,
        vit_down,
        adapter,
        text_rows,
        router,
        expert_ids,
        w_gate,
        w_up,
        w_down,
    ):
        vmem = pl.BlockSpec(memory_space=pltpu.VMEM)
        hbm = pl.BlockSpec(memory_space=pl.ANY)
        row_count, model = expert_ids.shape[0], adapter.shape[1]
        experts = router.shape[1]
        capacity = 7 * row_count // (8 * n_node)
        rows, width = patches.shape
        lanes = 128 * ((width // n_local + 127) // 128)
        slots = pl.pallas_call(
            lambda *refs: vision_kernel(n_local, capacity, *refs),
            out_shape=jax.ShapeDtypeStruct((experts, PAD, model), BF),
            in_specs=[vmem] * 8,
            out_specs=vmem,
            scratch_shapes=[
                pltpu.VMEM((n_local, rows, lanes), BF),
                pltpu.VMEM((n_local, rows, lanes), BF),
                pltpu.VMEM((n_local, rows, lanes), BF),
                pltpu.VMEM((n_local, 2 * rows // n_local, model // 2), BF),
                pltpu.VMEM((n_local, 2 * rows // n_local, model // 2), BF),
                pltpu.SemaphoreType.DMA((4, n_local)),
            ],
            compiler_params=pltpu.CompilerParams(
                collective_id=0,
                has_side_effects=True,
                vmem_limit_bytes=48 * 2**20,
            ),
        )(
            patches,
            norm_gain.reshape(1, -1),
            vit_up,
            vit_down,
            adapter,
            text_rows,
            router,
            expert_ids,
        )
        own_rows = n_node * capacity
        units = w_gate.shape[2]
        result = pl.pallas_call(
            lambda *refs: expert_kernel(n_node, capacity, *refs),
            out_shape=jax.ShapeDtypeStruct((own_rows, model), BF),
            in_specs=[vmem, hbm, hbm, hbm],
            out_specs=vmem,
            scratch_shapes=[
                pltpu.VMEM((model, units), BF),
                pltpu.VMEM((model, units), BF),
                pltpu.VMEM((units, model), BF),
                pltpu.VMEM((n_node, PAD, model), BF),
                pltpu.VMEM((n_local, own_rows, model), BF),
                pltpu.VMEM((n_local, own_rows, units), BF),
                pltpu.VMEM((5, 2, own_rows, model // 2), BF),
                pltpu.VMEM((5, 2, own_rows, model), BF),
                pltpu.SemaphoreType.DMA((4,)),
                pltpu.SemaphoreType.DMA((2, n_node)),
                pltpu.SemaphoreType.DMA((2, 5, 4)),
                pltpu.SemaphoreType.DMA((2, 5, 4)),
            ],
            compiler_params=pltpu.CompilerParams(
                collective_id=1,
                has_side_effects=True,
                vmem_limit_bytes=58 * 2**20,
            ),
        )(slots, w_gate, w_up, w_down)
        return result[None]

    return run


def solution(mesh):
    in_specs = (
        P("node", None),
        P(),
        P(None, "local"),
        P("local", None),
        P("local", None),
        P(("node", "local"), None),
        P(),
        P(("node", "local"), None),
        P("node", None, "local"),
        P("node", None, "local"),
        P("node", "local", None),
    )
    out_specs = P("node", "local", None)
    return jax.shard_map(
        on_device(mesh.shape["node"], mesh.shape["local"]),
        mesh=mesh,
        in_specs=in_specs,
        out_specs=out_specs,
        check_vma=False,
    )
```

```python
import functools

import jax
import jax.numpy as jnp
from jax import lax
from jax.experimental import pallas as pl
from jax.experimental.pallas import tpu as pltpu
from jax.sharding import PartitionSpec as P

MESH = pl.DeviceIdType.MESH
BF = jnp.bfloat16
F32 = jnp.float32
SIDE = 4
PAD = 16


def remote(src, dst, send_sem, recv_sem, device):
    return pltpu.make_async_remote_copy(
        src_ref=src,
        dst_ref=dst,
        send_sem=send_sem,
        recv_sem=recv_sem,
        device_id=device,
        device_id_type=MESH,
    )


def greet(devices):
    barrier = pltpu.get_barrier_semaphore()
    for device in devices:
        pl.semaphore_signal(barrier, inc=1, device_id=device, device_id_type=MESH)
    pl.semaphore_wait(barrier, len(devices))


def vision_kernel(
    n_node,
    n_local,
    capacity,
    patches_ref,
    gain_ref,
    up_ref,
    down_ref,
    adapter_ref,
    text_ref,
    router_ref,
    ids_ref,
    gate_hbm,
    up_hbm,
    down_hbm,
    out_ref,
    gate_swap,
    up_swap,
    down_swap,
    slots,
    arrived,
    part_send,
    part_recv,
    patch_blocks,
    embed_send,
    embed_recv,
    sems,
    node_sem,
    swap_sem,
):
    node, local = lax.axis_index("node"), lax.axis_index("local")
    peers = [(node, lax.rem(local + k, n_local)) for k in range(1, n_local)]
    core = lax.rem(node, 2)
    x, y = local // SIDE, lax.rem(local, SIDE)
    column = [(lax.rem(node + k, n_node), local) for k in range(1, n_node)]
    sibling = node + 1 - 2 * core
    beside = [(sibling, lax.rem(x + d, SIDE) * SIDE + y) for d in (SIDE - 1, 1)]
    greet(peers + column + beside)

    units = gate_hbm.shape[2]
    swaps = []
    for way in range(2):
        part = pl.ds(way * (units // 2), units // 2)
        for index, (here, there) in enumerate(
            (
                (gate_hbm.at[0, :, part], gate_swap.at[:, part]),
                (up_hbm.at[0, :, part], up_swap.at[:, part]),
                (down_hbm.at[0, part, :], down_swap.at[part, :]),
            )
        ):
            swaps.append(
                remote(
                    here,
                    there,
                    swap_sem.at[0, way, index],
                    swap_sem.at[1, way, index],
                    beside[way],
                )
            )

    @pl.when(core != lax.rem(x, 2))
    def _():
        for copy in swaps:
            copy.start()

    rows, width = patches_ref.shape
    block = width // n_local
    values = patches_ref[...].astype(F32)
    center = jnp.mean(values, axis=-1, keepdims=True)
    spread = jnp.mean((values - center) ** 2, axis=-1, keepdims=True)
    normed = ((values - center) * lax.rsqrt(spread + 1e-05) * gain_ref[...]).astype(BF)
    inner = jax.nn.gelu(
        jnp.dot(normed, up_ref[...], preferred_element_type=F32), approximate=True
    ).astype(BF)
    partial_sum = jnp.dot(inner, down_ref[...], preferred_element_type=F32)
    for index in range(n_local):
        low = index * block
        part_send[index, :, 0:block] = partial_sum[:, low : low + block].astype(BF)
        patch_blocks[index, :, 0:block] = values[:, low : low + block].astype(BF)

    first = []
    for k in range(1, n_local):
        copy = remote(
            part_send.at[peers[k - 1][1]],
            part_recv.at[k],
            sems.at[0, k],
            sems.at[1, k],
            peers[k - 1],
        )
        copy.start()
        first.append(copy)

    text_rows, model = text_ref.shape
    all_rows = ids_ref.shape[0]
    experts = router_ref.shape[1]
    chosen = ids_ref[...]
    table = (
        chosen == lax.broadcasted_iota(jnp.int32, (all_rows, experts), 1)
    ).astype(F32)
    earlier = (
        lax.broadcasted_iota(jnp.int32, (all_rows, all_rows), 0)
        > lax.broadcasted_iota(jnp.int32, (all_rows, all_rows), 1)
    ).astype(BF)
    counts = jnp.dot(earlier, table.astype(BF), preferred_element_type=F32)
    rank = jnp.sum(counts * table, axis=1, keepdims=True).astype(jnp.int32)
    slot = jnp.where(rank < capacity, chosen * PAD + rank, -1)
    place = jnp.transpose(
        (slot == lax.broadcasted_iota(jnp.int32, (all_rows, experts * PAD), 1)).astype(F32)
    ).astype(BF)
    logits = jnp.dot(text_ref[...], router_ref[...], preferred_element_type=F32)
    score = jax.nn.sigmoid(
        jnp.sum(logits * table[0:text_rows], axis=1, keepdims=True)
    )
    step = 512

    half = model // 2

    def place_text(part, index, carry):
        low = pl.multiple_of(index * step, step)
        columns = pl.ds(pl.multiple_of(part * half + low, step), step)
        scaled = text_ref[:, columns].astype(F32) * score
        scaled = jnp.concatenate(
            [scaled, jnp.zeros((all_rows - text_rows, step), F32)], axis=0
        ).astype(BF)
        sent = jnp.dot(place, scaled, preferred_element_type=F32).astype(BF)
        for expert in range(experts):
            slots[part, expert, :, pl.ds(low, step)] = sent[expert * PAD : (expert + 1) * PAD]
        return carry

    for part in range(2):
        lax.fori_loop(0, half // step, functools.partial(place_text, part), 0)

    total = part_send[local, :, 0:block].astype(F32)
    for k in range(1, n_local):
        first[k - 1].wait_recv()
        total = total + part_recv[k, :, 0:block].astype(F32)
    vision = (patch_blocks[local, :, 0:block].astype(F32) + total).astype(BF)

    own = rows // n_local
    wide = 640

    def embed_part(index, carry):
        low = pl.ds(pl.multiple_of(index * wide, 128), wide)
        high = pl.ds(pl.multiple_of(index * wide + half, 128), wide)
        left = jnp.dot(vision, adapter_ref[:, low], preferred_element_type=F32)
        right = jnp.dot(vision, adapter_ref[:, high], preferred_element_type=F32)
        for j in range(n_local):
            embed_send[j, :, low] = jnp.concatenate(
                [left[j * own : (j + 1) * own], right[j * own : (j + 1) * own]], axis=0
            ).astype(BF)
        return carry

    lax.fori_loop(0, half // wide, embed_part, 0)

    second = []
    for k in range(1, n_local):
        copy = remote(
            embed_send.at[peers[k - 1][1]],
            embed_recv.at[k],
            sems.at[2, k],
            sems.at[3, k],
            peers[k - 1],
        )
        copy.start()
        second.append(copy)
    for k in range(1, n_local):
        second[k - 1].wait_recv()

    embed = embed_send[local].astype(F32)
    for k in range(1, n_local):
        embed = embed + embed_recv[k].astype(F32)
    embed = embed.astype(BF).astype(F32)
    image = jnp.dot(
        embed[0:own].astype(BF), router_ref[0:half, :], preferred_element_type=F32
    ) + jnp.dot(
        embed[own : 2 * own].astype(BF), router_ref[half:model, :], preferred_element_type=F32
    )
    image_score = jax.nn.sigmoid(
        jnp.sum(image * table[text_rows:all_rows], axis=1, keepdims=True)
    )
    for part in range(2):
        for low in range(0, half, step):
            scaled = embed[part * own : (part + 1) * own, low : low + step] * image_score
            scaled = jnp.concatenate(
                [jnp.zeros((text_rows, step), F32), scaled], axis=0
            ).astype(BF)
            sent = jnp.dot(place, scaled, preferred_element_type=F32)
            for expert in range(experts):
                slots[part, expert, :, low : low + step] = (
                    slots[part, expert, :, low : low + step].astype(F32)
                    + sent[expert * PAD : (expert + 1) * PAD]
                ).astype(BF)

    third = []
    for k in range(1, n_node):
        target = column[k - 1][0]
        copy = remote(
            slots.at[lax.rem(target, 2), pl.ds(target // 2 * 2, 2)],
            arrived.at[node],
            node_sem.at[0, k],
            node_sem.at[1, k],
            column[k - 1],
        )
        copy.start()
        third.append(copy)
    mine = pltpu.make_async_copy(
        slots.at[core, pl.ds(node // 2 * 2, 2)], arrived.at[node], node_sem.at[0, 0]
    )
    mine.start()
    for k in range(1, n_node):
        source = arrived.at[lax.rem(node + n_node - k, n_node)]
        remote(source, source, node_sem.at[0, k], node_sem.at[1, k], column[k - 1]).wait_recv()
    mine.wait()

    kept = out_ref.shape[1]
    wanted = lax.broadcasted_iota(jnp.int32, (kept, n_node * PAD), 0)
    origin = lax.broadcasted_iota(jnp.int32, (kept, n_node * PAD), 1)
    pick = (wanted // capacity * PAD + lax.rem(wanted, capacity) == origin).astype(BF)

    def compact(expert, index, carry):
        columns = pl.ds(pl.multiple_of(index * step, step), step)
        out_ref[expert, :, columns] = jnp.dot(
            pick,
            arrived[:, expert, :, columns].reshape(n_node * PAD, step),
            preferred_element_type=F32,
        ).astype(BF)
        return carry

    for expert in range(2):
        lax.fori_loop(0, half // step, functools.partial(compact, expert), 0)

    for copy in first + second + third:
        copy.wait_send()

    @pl.when(core != lax.rem(x, 2))
    def _():
        for copy in swaps:
            copy.wait()


def wrap(p):
    return lax.rem(p + SIDE, SIDE)


def expert_kernel(
    own_ref,
    gate_hbm,
    up_hbm,
    down_hbm,
    gate_swap,
    up_swap,
    down_swap,
    out_ref,
    gate_ref,
    up_ref,
    down_ref,
    held,
    foreign,
    total,
    hidden,
    inner,
    r_half,
    r_full,
    x_recv,
    last,
    load_sem,
    ring_sem,
    cross_sem,
    chip_sem,
    r_ring_sem,
    r_cross_sem,
    r_chip_sem,
    last_sem,
):
    node, local = lax.axis_index("node"), lax.axis_index("local")
    core = lax.rem(node, 2)
    x, y = local // SIDE, lax.rem(local, SIDE)
    kind = lax.rem(x, 2)
    rows, width = held.shape[2], held.shape[3]
    half = width // 2
    units = hidden.shape[2]
    sibling = (node + 1 - 2 * core, local)

    def device(dx, dy):
        return (node, wrap(x + dx) * SIDE + wrap(y + dy))

    def blk(dx, dy):
        return wrap(x + dx) * SIDE + wrap(y + dy)

    greet([sibling, device(1, 0), device(-1, 0), device(2, 0), device(0, 1), device(0, -1)])

    wanted = (gate_ref, up_ref, down_ref)

    @pl.when(core == kind)
    def _():
        for index, source in enumerate((gate_hbm, up_hbm, down_hbm)):
            pltpu.make_async_copy(source.at[0], wanted[index], load_sem.at[index]).start()

    @pl.when(core != kind)
    def _():
        for index, source in enumerate((gate_swap, up_swap, down_swap)):
            pltpu.make_async_copy(source, wanted[index], load_sem.at[index]).start()

    def loaded(index):
        source = (gate_swap, up_swap, down_swap)[index]
        pltpu.make_async_copy(source, wanted[index], load_sem.at[index]).wait()

    def run(c):
        pending = {}

        def launch(key, copy):
            copy.start()
            pending.setdefault(key, []).append(copy)

        def settle(key):
            for copy in pending.pop(key, []):
                copy.wait_send()

        def key_of(dx, dy):
            return (dx % SIDE, dy % SIDE)

        held[c, blk(0, 0)] = own_ref[kind]
        foreign[wrap(y)] = own_ref[1 - kind]

        def chip_copy(cls, dx, dy):
            ref = held.at[cls, blk(dx, dy)]
            i = dx % SIDE * SIDE + dy % SIDE
            return remote(ref, ref, chip_sem.at[0, i], chip_sem.at[1, i], sibling)

        def share(dx, dy):
            launch(key_of(dx, dy), chip_copy(c, dx, dy))

        def slot(op, dy, columns):
            if c == 0:
                return held.at[0, blk(op, dy), :, columns], key_of(op, dy)
            if op == 0:
                return held.at[1, blk(0, dy), :, columns], key_of(0, dy)
            return foreign.at[wrap(y + dy), :, columns], ("F", dy % SIDE)

        def y_copy(op, way, dy, is_half):
            columns = pl.ds(way * half, half) if is_half else pl.ds(0, width)
            ref, key = slot(op, dy, columns)
            sem = 2 * is_half + way
            return key, remote(
                ref,
                ref,
                ring_sem.at[0, op, sem],
                ring_sem.at[1, op, sem],
                device(0, (1, -1)[way]),
            )

        def y_start(op):
            for way in range(2):
                launch(*y_copy(op, way, 0, False))

        def y_full_recv(op, way):
            dy = (-1, 1)[way]
            y_copy(op, way, dy, False)[1].wait_recv()
            launch(*y_copy(op, way, dy, True))

        def y_half_recv(op):
            for way in range(2):
                y_copy(op, way, 2, True)[1].wait_recv()

        def cross_send(dy):
            s = dy % SIDE
            there = held.at[c, blk(0, dy)]
            for way in range(2):
                launch(
                    ("F", s),
                    remote(
                        foreign.at[wrap(y + dy)],
                        there,
                        cross_sem.at[0, s, way],
                        cross_sem.at[1, s, way],
                        device((1, -1)[way], 0),
                    ),
                )
            launch(
                key_of(0, dy),
                remote(there, there, cross_sem.at[0, s, 2], cross_sem.at[1, s, 2], device(2, 0)),
            )

        def cross_recv(dy, way):
            s = dy % SIDE
            ref = held.at[c, blk((-1, 1, 2)[way], dy)]
            remote(
                ref, ref, cross_sem.at[0, s, way], cross_sem.at[1, s, way], device(2, 0)
            ).wait_recv()

        depth = 1280
        done = {}

        def unit(cls, block, ends):
            def body(index, carry):
                gate, upper = carry
                low = pl.multiple_of(index * depth, depth)
                deep = pl.ds(pl.multiple_of(cls * width + low, depth), depth)
                piece = held[cls, block, :, pl.ds(low, depth)]
                return (
                    gate + jnp.dot(piece, gate_ref[deep, :], preferred_element_type=F32),
                    upper + jnp.dot(piece, up_ref[deep, :], preferred_element_type=F32),
                )

            if ends:
                start = (total[block, :, 0:units], total[block, :, units : 2 * units])
            else:
                start = (jnp.zeros((rows, units), F32), jnp.zeros((rows, units), F32))
            gate, upper = lax.fori_loop(0, width // depth, body, start)
            if ends:
                hidden[block] = (jax.nn.silu(gate) * upper).astype(BF)
            else:
                total[block, :, 0:units] = gate
                total[block, :, units : 2 * units] = upper

        def compute(cls, places):
            if cls != c:
                for place in places:
                    chip_copy(cls, *place).wait_recv()
            for ends in (False, True):
                group = [p for p in places if (key_of(*p) in done) == ends]
                if not group:
                    continue

                def body(index, carry):
                    block = blk(*group[0])
                    for number in range(1, len(group)):
                        block = jnp.where(index == number, blk(*group[number]), block)
                    unit(cls, block, ends)
                    return carry

                if len(group) == 1:
                    body(0, 0)
                else:
                    lax.fori_loop(0, len(group), body, 0)
            for place in places:
                done[key_of(*place)] = True

        beside_y = [(0, -1), (0, 1)]
        if c == 0:
            cross_send(0)
            y_start(0)
            share(0, 0)
            loaded(0)
            loaded(1)
            compute(0, [(0, 0)])
            compute(1, [(0, 0)])
            for way in range(2):
                y_full_recv(0, way)
                share(*beside_y[way])
            compute(0, beside_y)
            compute(1, beside_y)
            for way, dx in enumerate((-1, 1, 2)):
                cross_recv(0, way)
                y_start(dx % SIDE)
                share(dx, 0)
            compute(0, [(-1, 0), (1, 0), (2, 0)])
            y_half_recv(0)
            share(0, 2)
            compute(1, [(-1, 0), (1, 0), (2, 0)])
            compute(0, [(0, 2)])
            compute(1, [(0, 2)])
            for dx in (-1, 1, 2):
                for way in range(2):
                    y_full_recv(dx % SIDE, way)
                    share(dx, (-1, 1)[way])
                compute(0, [(dx, -1), (dx, 1)])
                if dx != 2:
                    compute(1, [(-1, dx), (1, dx), (2, dx)])
            for dx in (-1, 1):
                y_half_recv(dx % SIDE)
                share(dx, 2)
                compute(0, [(dx, 2)])
            y_half_recv(2)
            share(2, 2)
            compute(0, [(2, 2)])
            compute(1, [(-1, 2), (1, 2), (2, 2)])
        else:
            y_start(0)
            y_start(1)
            cross_send(0)
            share(0, 0)
            loaded(0)
            loaded(1)
            compute(1, [(0, 0)])
            compute(0, [(0, 0)])
            for way in range(2):
                for op in range(2):
                    y_full_recv(op, way)
                cross_send((-1, 1)[way])
                share(*beside_y[way])
            compute(1, beside_y)
            compute(0, beside_y)
            for way, dx in enumerate((-1, 1, 2)):
                cross_recv(0, way)
                share(dx, 0)
            compute(1, [(-1, 0), (1, 0), (2, 0)])
            for op in range(2):
                y_half_recv(op)
            cross_send(2)
            share(0, 2)
            compute(0, [(-1, 0), (1, 0), (2, 0)])
            compute(1, [(0, 2)])
            compute(0, [(0, 2)])
            for dy in (-1, 1):
                for way, dx in enumerate((-1, 1, 2)):
                    cross_recv(dy, way)
                    share(dx, dy)
                compute(1, [(-1, dy), (1, dy), (2, dy)])
                compute(0, [(dy, -1), (dy, 1)])
            compute(0, [(2, -1), (2, 1)])
            compute(0, [(-1, 2), (1, 2)])
            for way, dx in enumerate((-1, 1, 2)):
                cross_recv(2, way)
                share(dx, 2)
            compute(1, [(-1, 2), (1, 2), (2, 2)])
            compute(0, [(2, 2)])

        loaded(2)
        step = 640

        def product(cls, block, dest, terms):
            for part in range(2):

                def body(index, carry):
                    low = pl.multiple_of(index * step, 128)
                    here = pl.multiple_of(low + part * half, 128)
                    columns = pl.ds(here, step)
                    value = None
                    if block is not None:
                        value = jnp.dot(
                            hidden[block],
                            down_ref[:, pl.ds(pl.multiple_of(here + cls * width, 128), step)],
                            preferred_element_type=F32,
                        )
                    for get, which in terms:
                        if which is None:
                            term = get(columns).astype(F32)
                        elif which == part:
                            term = get(pl.ds(low, step)).astype(F32)
                        else:
                            continue
                        value = term if value is None else value + term
                    dest[:, columns] = value.astype(BF)
                    return carry

                lax.fori_loop(0, half // step, body, 0)

        orders = (
            [(2, 2), (1, 2), (-1, 2), (0, 2), (2, 1), (2, -1), (1, 1), (1, -1), (2, 0)]
            + [(-1, 1), (-1, -1), (1, 0), (0, 1), (0, -1), (-1, 0), (0, 0)],
            [(2, 2), (1, 2), (-1, 2), (2, 1), (1, 1), (-1, 1), (0, 2), (2, -1), (1, -1)]
            + [(-1, -1), (0, 1), (2, 0), (1, 0), (-1, 0), (0, -1), (0, 0)],
        )
        queue = list(orders[1 - c])

        def inner_copy(cls, dx, dy):
            i = dx % SIDE * SIDE + dy % SIDE
            return remote(
                held.at[cls, blk(dx, dy)],
                inner.at[blk(dx, dy)],
                r_chip_sem.at[0, i],
                r_chip_sem.at[1, i],
                sibling,
            )

        def feed():
            if queue:
                dx, dy = queue.pop(0)
                block = blk(dx, dy)
                product(1 - c, block, held.at[1 - c, block], ())
                launch(("chip", dx, dy), inner_copy(1 - c, dx, dy))

        served = []

        def chip_sum(dx, dy, terms):
            served.append((dx, dy))
            block = blk(dx, dy)
            inner_copy(c, dx, dy).wait_recv()
            settle(key_of(dx, dy))
            product(
                c,
                block,
                held.at[c, block],
                [(lambda columns: inner[block, :, columns], None)] + terms,
            )
            feed()

        def ring_back(op, way, ref, is_half):
            if is_half:
                return remote(
                    ref.at[:, pl.ds(way * half, half)],
                    r_half.at[op, way],
                    r_ring_sem.at[0, op, way],
                    r_ring_sem.at[1, op, way],
                    device(0, (1, -1)[way]),
                )
            return remote(
                ref,
                r_full.at[op, way],
                r_ring_sem.at[0, op, 2 + way],
                r_ring_sem.at[1, op, 2 + way],
                device(0, (1, -1)[way]),
            )

        def half_term(op, way):
            ring_back(op, way, held.at[c, 0], True).wait_recv()
            return (lambda columns: r_half[op, way, :, columns], way)

        def full_terms(op):
            for way in range(2):
                ring_back(op, way, held.at[c, 0], False).wait_recv()
            return [
                (lambda columns: r_full[op, 0, :, columns], None),
                (lambda columns: r_full[op, 1, :, columns], None),
            ]

        def cross_back(s, way, ref):
            return remote(
                ref,
                x_recv.at[s, way],
                r_cross_sem.at[0, s, way],
                r_cross_sem.at[1, s, way],
                device((1, -1, 2)[way], 0),
            )

        def cross_term(s, way):
            cross_back(s, way, held.at[c, 0]).wait_recv()
            return (lambda columns: x_recv[s, way, :, columns], None)

        ours, theirs = held.at[c, blk(0, 0)], foreign.at[wrap(y)]
        feed()
        feed()
        if c == 0:

            def far(dx):
                chip_sum(dx, 2, [])
                for way in range(2):
                    launch("back", ring_back(dx % SIDE, way, held.at[0, blk(dx, 2)], True))

            def near(dx):
                for way in range(2):
                    dy = (1, -1)[way]
                    chip_sum(dx, dy, [half_term(dx % SIDE, way)])
                    launch("back", ring_back(dx % SIDE, way, held.at[0, blk(dx, dy)], False))

            def home(dx):
                terms = full_terms(dx % SIDE)
                if dx == 0:
                    terms.append(cross_term(0, 2))
                chip_sum(dx, 0, terms)
                if dx != 0:
                    way = {1: 0, -1: 1, 2: 2}[dx]
                    launch("back", cross_back(0, way, held.at[0, blk(dx, 0)]))

            for dx in (2, 1, -1, 0):
                far(dx)
            near(2)
            near(1)
            home(2)
            near(-1)
            home(1)
            near(0)
            home(-1)
            home(0)
            settle(("F", 0))
            product(0, None, theirs, [cross_term(0, 0), cross_term(0, 1)])
        else:

            def away(dy):
                for way, dx in ((2, 2), (0, 1), (1, -1)):
                    chip_sum(dx, dy, [])
                    launch("back", cross_back(dy % SIDE, way, held.at[1, blk(dx, dy)]))

            def home(dy):
                s = dy % SIDE
                extra = ([], [])
                for op in range(2):
                    if dy in (1, -1):
                        extra[op].append(half_term(op, (1, -1).index(dy)))
                    if dy == 0:
                        extra[op].extend(full_terms(op))
                chip_sum(0, dy, [cross_term(s, 2)] + extra[0])
                settle(("F", s))
                other = foreign.at[wrap(y + dy)]
                product(1, None, other, [cross_term(s, 0), cross_term(s, 1)] + extra[1])
                for op, ref in enumerate((held.at[1, blk(0, dy)], other)):
                    if dy == 2:
                        for way in range(2):
                            launch("back", ring_back(op, way, ref, True))
                    elif dy != 0:
                        launch("back", ring_back(op, (1, -1).index(dy), ref, False))

            away(2)
            away(1)
            home(2)
            away(-1)
            home(1)
            away(0)
            home(-1)
            home(0)
        assert served == orders[c] and not queue

        here, there = pl.ds(c * width, width), pl.ds((1 - c) * width, width)

        def finish(keep, give):
            copy = remote(give, last, last_sem.at[0], last_sem.at[1], sibling)
            copy.start()
            out_ref[:, here] = keep[...]
            copy.wait()

        @pl.when(kind == c)
        def _():
            finish(ours, theirs)

        @pl.when(kind != c)
        def _():
            finish(theirs, ours)

        out_ref[:, there] = last[...]
        for key in list(pending):
            settle(key)

    for c in range(2):
        pl.when(core == c)(functools.partial(run, c))


def on_device(n_node, n_local):
    def run(
        patches,
        norm_gain,
        vit_up,
        vit_down,
        adapter,
        text_rows,
        router,
        expert_ids,
        w_gate,
        w_up,
        w_down,
    ):
        vmem = pl.BlockSpec(memory_space=pltpu.VMEM)
        hbm = pl.BlockSpec(memory_space=pl.ANY)
        row_count, model = expert_ids.shape[0], adapter.shape[1]
        experts = router.shape[1]
        capacity = 7 * row_count // (8 * n_node)
        rows, width = patches.shape
        lanes = 128 * ((width // n_local + 127) // 128)
        own_rows = n_node * capacity
        units = w_gate.shape[2]
        half = model // 2
        swapped = [jax.ShapeDtypeStruct(w.shape[1:], BF) for w in (w_gate, w_up, w_down)]
        own, gate_swap, up_swap, down_swap = pl.pallas_call(
            functools.partial(vision_kernel, n_node, n_local, capacity),
            out_shape=[jax.ShapeDtypeStruct((2, own_rows, half), BF)] + swapped,
            in_specs=[vmem] * 8 + [hbm] * 3,
            out_specs=[vmem] + [hbm] * 3,
            scratch_shapes=[
                pltpu.VMEM((2, experts, PAD, half), BF),
                pltpu.VMEM((n_node, 2, PAD, half), BF),
                pltpu.VMEM((n_local, rows, lanes), BF),
                pltpu.VMEM((n_local, rows, lanes), BF),
                pltpu.VMEM((n_local, rows, lanes), BF),
                pltpu.VMEM((n_local, 2 * rows // n_local, half), BF),
                pltpu.VMEM((n_local, 2 * rows // n_local, half), BF),
                pltpu.SemaphoreType.DMA((4, n_local)),
                pltpu.SemaphoreType.DMA((2, n_node)),
                pltpu.SemaphoreType.DMA((2, 2, 3)),
            ],
            compiler_params=pltpu.CompilerParams(
                collective_id=0,
                has_side_effects=True,
                vmem_limit_bytes=48 * 2**20,
            ),
        )(
            patches,
            norm_gain.reshape(1, -1),
            vit_up,
            vit_down,
            adapter,
            text_rows,
            router,
            expert_ids,
            w_gate,
            w_up,
            w_down,
        )
        result = pl.pallas_call(
            expert_kernel,
            out_shape=jax.ShapeDtypeStruct((own_rows, model), BF),
            in_specs=[vmem] + [hbm] * 6,
            out_specs=vmem,
            scratch_shapes=[
                pltpu.VMEM((model, units), BF),
                pltpu.VMEM((model, units), BF),
                pltpu.VMEM((units, model), BF),
                pltpu.VMEM((2, n_local, own_rows, half), BF),
                pltpu.VMEM((SIDE, own_rows, half), BF),
                pltpu.VMEM((n_local, own_rows, 2 * units), F32),
                pltpu.VMEM((n_local, own_rows, units), BF),
                pltpu.VMEM((n_local, own_rows, half), BF),
                pltpu.VMEM((SIDE, 2, own_rows, half // 2), BF),
                pltpu.VMEM((SIDE, 2, own_rows, half), BF),
                pltpu.VMEM((SIDE, 3, own_rows, half), BF),
                pltpu.VMEM((own_rows, half), BF),
                pltpu.SemaphoreType.DMA((3,)),
                pltpu.SemaphoreType.DMA((2, SIDE, 4)),
                pltpu.SemaphoreType.DMA((2, SIDE, 3)),
                pltpu.SemaphoreType.DMA((2, n_local)),
                pltpu.SemaphoreType.DMA((2, SIDE, 4)),
                pltpu.SemaphoreType.DMA((2, SIDE, 3)),
                pltpu.SemaphoreType.DMA((2, n_local)),
                pltpu.SemaphoreType.DMA((2,)),
            ],
            compiler_params=pltpu.CompilerParams(
                collective_id=1,
                has_side_effects=True,
                vmem_limit_bytes=60 * 2**20,
            ),
        )(own, w_gate, w_up, w_down, gate_swap, up_swap, down_swap)
        return result[None]

    return run


def solution(mesh):
    in_specs = (
        P("node", None),
        P(),
        P(None, "local"),
        P("local", None),
        P("local", None),
        P(("node", "local"), None),
        P(),
        P(("node", "local"), None),
        P("node", None, "local"),
        P("node", None, "local"),
        P("node", "local", None),
    )
    out_specs = P("node", "local", None)
    return jax.shard_map(
        on_device(mesh.shape["node"], mesh.shape["local"]),
        mesh=mesh,
        in_specs=in_specs,
        out_specs=out_specs,
        check_vma=False,
    )
```

```python
import functools

import jax
import jax.numpy as jnp
from jax import lax
from jax.experimental import pallas as pl
from jax.experimental.pallas import tpu as pltpu
from jax.sharding import PartitionSpec as P

MESH = pl.DeviceIdType.MESH
BF = jnp.bfloat16
F32 = jnp.float32
SIDE = 4
PAD = 16
SWAP = (1, 3, 8)


def remote(src, dst, send_sem, recv_sem, device):
    return pltpu.make_async_remote_copy(
        src_ref=src,
        dst_ref=dst,
        send_sem=send_sem,
        recv_sem=recv_sem,
        device_id=device,
        device_id_type=MESH,
    )


def greet(devices):
    barrier = pltpu.get_barrier_semaphore()
    for device in devices:
        pl.semaphore_signal(barrier, inc=1, device_id=device, device_id_type=MESH)
    pl.semaphore_wait(barrier, len(devices))


def vision_kernel(
    n_node,
    n_local,
    capacity,
    share,
    patches_hbm,
    gain_ref,
    vit_up_hbm,
    vit_down_hbm,
    adapter_hbm,
    text_hbm,
    router_ref,
    ids_ref,
    gate_hbm,
    up_hbm,
    out_ref,
    gate_swap,
    up_swap,
    patches_ref,
    up_ref,
    down_ref,
    adapter_ref,
    text_ref,
    load_sem,
    slots,
    arrived,
    image_send,
    image_recv,
    part_send,
    part_recv,
    patch_blocks,
    embed_send,
    embed_recv,
    sems,
    node_sem,
    swap_sem,
):
    node, local = lax.axis_index("node"), lax.axis_index("local")
    peers = [(node, lax.rem(local + k, n_local)) for k in range(1, n_local)]
    core = lax.rem(node, 2)
    x, y = local // SIDE, lax.rem(local, SIDE)
    column = [(lax.rem(node + k, n_node), local) for k in range(1, n_node)]
    sibling = node + 1 - 2 * core
    beside = [(sibling, lax.rem(x + d, SIDE) * SIDE + y) for d in (SIDE - 1, 1)]
    loads = [
        pltpu.make_async_copy(source, ref, load_sem.at[index])
        for index, (source, ref) in enumerate(
            (
                (patches_hbm, patches_ref),
                (vit_up_hbm, up_ref),
                (vit_down_hbm, down_ref),
                (text_hbm, text_ref),
                (adapter_hbm, adapter_ref),
            )
        )
    ]
    for load in loads:
        load.start()
    barrier = pltpu.get_barrier_semaphore()
    for device in peers + column + beside:
        pl.semaphore_signal(barrier, inc=1, device_id=device, device_id_type=MESH)

    units, model = gate_hbm.shape[2], gate_hbm.shape[1]
    swaps = []
    for index, (here, there) in enumerate(((gate_hbm, gate_swap), (up_hbm, up_swap))):
        for quarter in range(4):
            deep = pl.ds(quarter * (model // 4), model // 4)
            for way in range(2):
                part = pl.ds(way * (units // 2), units // 2)
                swaps.append(
                    remote(
                        here.at[0, deep, part],
                        there.at[deep, part],
                        swap_sem.at[0, way, index * 4 + quarter],
                        swap_sem.at[1, way, index * 4 + quarter],
                        beside[way],
                    )
                )

    def swap(low, high):
        @pl.when(core != lax.rem(x, 2))
        def _():
            for copy in swaps[2 * low : 2 * high]:
                copy.start()

    rows, width = patches_ref.shape
    block = width // n_local
    loads[0].wait()
    values = patches_ref[...].astype(F32)
    center = jnp.mean(values, axis=-1, keepdims=True)
    spread = jnp.mean((values - center) ** 2, axis=-1, keepdims=True)
    normed = ((values - center) * lax.rsqrt(spread + 1e-05) * gain_ref[...]).astype(BF)
    pl.semaphore_wait(barrier, len(peers + column + beside))
    swap(0, SWAP[0])
    last_dims = (((1,), (1,)), ((), ()))
    loads[1].wait()
    loads[2].wait()
    inner = jax.nn.gelu(
        lax.dot_general(normed, up_ref[...], last_dims, preferred_element_type=F32),
        approximate=True,
    ).astype(BF)
    partial_sum = jnp.dot(inner, down_ref[...], preferred_element_type=F32)
    for index in range(n_local):
        low = index * block
        part_send[index, :, 0:block] = partial_sum[:, low : low + block].astype(BF)

    first = []
    for k in range(1, n_local):
        copy = remote(
            part_send.at[peers[k - 1][1]],
            part_recv.at[k],
            sems.at[0, k],
            sems.at[1, k],
            peers[k - 1],
        )
        copy.start()
        first.append(copy)
    swap(SWAP[0], SWAP[1])

    for index in range(n_local):
        low = index * block
        patch_blocks[index, :, 0:block] = values[:, low : low + block].astype(BF)
    text_rows = text_ref.shape[0]
    all_rows = ids_ref.shape[1]
    experts = router_ref.shape[0]
    square = (all_rows, all_rows)
    chosen = jnp.transpose(jnp.broadcast_to(ids_ref[...].astype(F32), square))[:, 0:1]
    table = (
        chosen == lax.broadcasted_iota(jnp.int32, (all_rows, experts), 1).astype(F32)
    ).astype(F32)
    earlier = (
        lax.broadcasted_iota(jnp.int32, square, 0) > lax.broadcasted_iota(jnp.int32, square, 1)
    ).astype(BF)
    counts = jnp.dot(earlier, table.astype(BF), preferred_element_type=F32)
    rank = jnp.sum(counts * table, axis=1, keepdims=True)
    slot = jnp.where(rank < capacity, chosen * PAD + rank, -1.0).astype(jnp.int32)
    place = jnp.transpose(
        (slot == lax.broadcasted_iota(jnp.int32, (all_rows, experts * PAD), 1)).astype(F32)
    ).astype(BF)
    loads[3].wait()
    logits = lax.dot_general(
        text_ref[...], router_ref[...], last_dims, preferred_element_type=F32
    )
    score = jax.nn.sigmoid(jnp.sum(logits * table[0:text_rows], axis=1, keepdims=True))
    step = 512
    shares = (share, model - share)

    def place_text(part, index, carry):
        low = pl.multiple_of(index * step, step)
        columns = pl.ds(pl.multiple_of(part * share + low, step), step)
        scaled = text_ref[:, columns].astype(F32) * score
        scaled = jnp.concatenate(
            [scaled, jnp.zeros((all_rows - text_rows, step), F32)], axis=0
        ).astype(BF)
        sent = jnp.dot(place, scaled, preferred_element_type=F32).astype(BF)
        for expert in range(experts):
            slots[part, expert, :, pl.ds(low, step)] = sent[expert * PAD : (expert + 1) * PAD]
        return carry

    for part in range(2):
        lax.fori_loop(0, shares[part] // step, functools.partial(place_text, part), 0)
        for expert in range(experts):
            slots[part, expert, :, share : share + all_rows] = place[
                expert * PAD : (expert + 1) * PAD
            ]

    def to_column(source_of, there, sem):
        copies = []
        for k in range(1, n_node):
            copy = remote(
                source_of(column[k - 1][0]),
                there.at[node],
                node_sem.at[sem, k],
                node_sem.at[sem + 1, k],
                column[k - 1],
            )
            copy.start()
            copies.append(copy)
        mine = pltpu.make_async_copy(source_of(node), there.at[node], node_sem.at[sem, 0])
        mine.start()

        def arrive():
            for k in range(1, n_node):
                source = there.at[lax.rem(node + n_node - k, n_node)]
                remote(
                    source, source, node_sem.at[sem, k], node_sem.at[sem + 1, k], column[k - 1]
                ).wait_recv()
            mine.wait()

        return copies, arrive

    third, text_arrives = to_column(
        lambda target: slots.at[lax.rem(target, 2), pl.ds(target // 2 * 2, 2)], arrived, 0
    )

    total = part_send[local, :, 0:block].astype(F32)
    for k in range(1, n_local):
        first[k - 1].wait_recv()
        total = total + part_recv[k, :, 0:block].astype(F32)
    vision = (patch_blocks[local, :, 0:block].astype(F32) + total).astype(BF)

    half = model // 2
    own = rows // n_local
    wide = 640

    loads[4].wait()

    def embed_part(index, carry):
        low = pl.ds(pl.multiple_of(index * wide, 128), wide)
        high = pl.ds(pl.multiple_of(index * wide + half, 128), wide)
        left = jnp.dot(vision, adapter_ref[:, low], preferred_element_type=F32)
        right = jnp.dot(vision, adapter_ref[:, high], preferred_element_type=F32)
        for j in range(n_local):
            embed_send[j, :, low] = jnp.concatenate(
                [left[j * own : (j + 1) * own], right[j * own : (j + 1) * own]], axis=0
            ).astype(BF)
        return carry

    lax.fori_loop(0, half // wide, embed_part, 0)

    second = []
    for k in range(1, n_local):
        copy = remote(
            embed_send.at[peers[k - 1][1]],
            embed_recv.at[k],
            sems.at[2, k],
            sems.at[3, k],
            peers[k - 1],
        )
        copy.start()
        second.append(copy)
    swap(SWAP[1], SWAP[2])
    for k in range(1, n_local):
        second[k - 1].wait_recv()

    embed = embed_send[local].astype(F32)
    for k in range(1, n_local):
        embed = embed + embed_recv[k].astype(F32)
    embed = embed.astype(BF).astype(F32)
    image = lax.dot_general(
        embed[0:own].astype(BF), router_ref[:, 0:half], last_dims, preferred_element_type=F32
    ) + lax.dot_general(
        embed[own : 2 * own].astype(BF),
        router_ref[:, half:model],
        last_dims,
        preferred_element_type=F32,
    )
    image_score = jax.nn.sigmoid(
        jnp.sum(image * table[text_rows:all_rows], axis=1, keepdims=True)
    )
    scaled = jnp.concatenate([embed[0:own], embed[own : 2 * own]], axis=1) * image_score
    for part in range(2):
        low, span = part * share, shares[part] // 2
        image_send[part, :, 0:span] = jnp.concatenate(
            [scaled[:, low : low + span], scaled[:, low + span : low + 2 * span]], axis=0
        ).astype(BF)
    fourth, image_arrives = to_column(
        lambda target: image_send.at[lax.rem(target, 2)], image_recv, 2
    )

    kept = out_ref.shape[1]
    wanted = lax.broadcasted_iota(jnp.int32, (kept, n_node * PAD), 0)
    origin = lax.broadcasted_iota(jnp.int32, (kept, n_node * PAD), 1)
    pick = (wanted // capacity * PAD + lax.rem(wanted, capacity) == origin).astype(BF)
    text_arrives()

    def compact(expert, index, carry):
        columns = pl.ds(pl.multiple_of(index * step, step), step)
        out_ref[expert, :, columns] = jnp.dot(
            pick,
            arrived[:, expert, :, columns].reshape(n_node * PAD, step),
            preferred_element_type=F32,
        ).astype(BF)
        return carry

    row = lax.broadcasted_iota(jnp.int32, (all_rows, n_node * PAD), 0)
    lane = lax.broadcasted_iota(jnp.int32, (all_rows, n_node * PAD), 1)
    same = (wanted // capacity == origin // PAD).astype(F32)
    spots = []
    for expert in range(2):
        lax.fori_loop(0, share // step, functools.partial(compact, expert), 0)
        places = jnp.dot(
            pick,
            arrived[:, expert, :, share : share + all_rows].reshape(n_node * PAD, all_rows),
            preferred_element_type=F32,
        ).astype(BF)
        for top in range(2):
            spread_rows = (
                (row - text_rows + top * own == lax.rem(lane, PAD)) & (row >= text_rows)
            ).astype(BF)
            spot = jnp.dot(places, spread_rows, preferred_element_type=F32) * same
            spots.append(spot.astype(BF))
    image_arrives()

    for c in range(2):

        @pl.when(core == c)
        def _(span=shares[c] // 2):
            for expert in range(2):
                for top in range(2):

                    def add(index, carry):
                        low = pl.multiple_of(index * step, step)
                        columns = pl.ds(pl.multiple_of(top * span + low, step), step)
                        image_rows = image_recv[:, :, pl.ds(low, step)]
                        out_ref[expert, :, columns] = (
                            out_ref[expert, :, columns].astype(F32)
                            + jnp.dot(
                                spots[2 * expert + top],
                                image_rows.reshape(n_node * PAD, step),
                                preferred_element_type=F32,
                            )
                        ).astype(BF)
                        return carry

                    lax.fori_loop(0, span // step, add, 0)

    for copy in first + second + third + fourth:
        copy.wait_send()

    @pl.when(core != lax.rem(x, 2))
    def _():
        for copy in swaps:
            copy.wait()


def wrap(p):
    return lax.rem(p + SIDE, SIDE)


def expert_kernel(
    own_ref,
    gate_hbm,
    up_hbm,
    down_hbm,
    gate_swap,
    up_swap,
    out_ref,
    gate_ref,
    up_ref,
    down_ref,
    held0,
    held1,
    foreign0,
    foreign1,
    total,
    hidden,
    inner,
    r_half,
    r_full,
    x_recv0,
    x_recv1,
    last,
    load_sem,
    swap_sem,
    ring_sem,
    cross_sem,
    chip_sem,
    r_ring_sem,
    r_cross_sem,
    r_chip_sem,
    last_sem,
):
    node, local = lax.axis_index("node"), lax.axis_index("local")
    core = lax.rem(node, 2)
    x, y = local // SIDE, lax.rem(local, SIDE)
    kind = lax.rem(x, 2)
    held = (held0, held1)
    widths = (held0.shape[2], held1.shape[2])
    offsets = (0, widths[0])
    rows = held0.shape[1]
    units = hidden.shape[2]
    sibling = (node + 1 - 2 * core, local)

    def device(dx, dy):
        return (node, wrap(x + dx) * SIDE + wrap(y + dy))

    def blk(dx, dy):
        return wrap(x + dx) * SIDE + wrap(y + dy)

    beside = [(sibling[0], device(d, 0)[1]) for d in (-1, 1)]
    greet(
        [sibling, device(1, 0), device(-1, 0), device(2, 0), device(0, 1), device(0, -1)] + beside
    )
    downs = [
        remote(
            down_hbm.at[0, pl.ds(way * (units // 2), units // 2), :],
            down_ref.at[pl.ds(way * (units // 2), units // 2), :],
            swap_sem.at[0, way],
            swap_sem.at[1, way],
            beside[way],
        )
        for way in range(2)
    ]
    own_down = pltpu.make_async_copy(down_hbm.at[0], down_ref, load_sem.at[2])

    @pl.when(core == kind)
    def _():
        for index, source in enumerate((gate_hbm, up_hbm)):
            ref = (gate_ref, up_ref)[index]
            pltpu.make_async_copy(source.at[0], ref, load_sem.at[index]).start()
        own_down.start()

    @pl.when(core != kind)
    def _():
        for index, source in enumerate((gate_swap, up_swap)):
            ref = (gate_ref, up_ref)[index]
            pltpu.make_async_copy(source, ref, load_sem.at[index]).start()

    def loaded(index):
        if index < 2:
            source, ref = ((gate_swap, gate_ref), (up_swap, up_ref))[index]
            pltpu.make_async_copy(source, ref, load_sem.at[index]).wait()
            return

        @pl.when(core == kind)
        def _():
            own_down.wait()

        @pl.when(core != kind)
        def _():
            for copy in downs:
                copy.wait()

    def swap_down():
        @pl.when(core != kind)
        def _():
            for copy in downs:
                copy.start()

    def run(c):
        pending = {}
        width = widths[c]
        half = width // 2

        def launch(key, copy):
            copy.start()
            pending.setdefault(key, []).append(copy)

        def settle(key):
            for copy in pending.pop(key, []):
                copy.wait_send()

        def key_of(dx, dy):
            return (dx % SIDE, dy % SIDE)

        def foreign(dy):
            return foreign0 if c == 0 else foreign1.at[wrap(y + dy)]

        pieces = [
            pltpu.make_async_copy(own_ref.at[index, :, pl.ds(0, width)], dest, load_sem.at[3 + n])
            for n, (index, dest) in enumerate(
                ((kind, held[c].at[blk(0, 0)]), (1 - kind, foreign(0)))
            )
        ]
        for piece in pieces:
            piece.start()
        for piece in pieces:
            piece.wait()

        def chip_copy(cls, dx, dy):
            ref = held[cls].at[blk(dx, dy)]
            i = dx % SIDE * SIDE + dy % SIDE
            return remote(ref, ref, chip_sem.at[0, i], chip_sem.at[1, i], sibling)

        def share(dx, dy):
            launch(key_of(dx, dy), chip_copy(c, dx, dy))

        def slot(op, dy, columns):
            if c == 0:
                return held0.at[blk(op, dy), :, columns], key_of(op, dy)
            if op == 0:
                return held1.at[blk(0, dy), :, columns], key_of(0, dy)
            return foreign1.at[wrap(y + dy), :, columns], ("F", dy % SIDE)

        def y_copy(op, way, dy, is_half):
            columns = pl.ds(way * half, half) if is_half else pl.ds(0, width)
            ref, key = slot(op, dy, columns)
            sem = 2 * is_half + way
            return key, remote(
                ref,
                ref,
                ring_sem.at[0, op, sem],
                ring_sem.at[1, op, sem],
                device(0, (1, -1)[way]),
            )

        def y_start(op):
            for way in range(2):
                launch(*y_copy(op, way, 0, False))

        def y_full_recv(op, way):
            dy = (-1, 1)[way]
            y_copy(op, way, dy, False)[1].wait_recv()
            launch(*y_copy(op, way, dy, True))

        def y_half_recv(op):
            for way in range(2):
                y_copy(op, way, 2, True)[1].wait_recv()

        def cross_send(dy):
            s = dy % SIDE
            there = held[c].at[blk(0, dy)]
            for way in range(2):
                launch(
                    ("F", s),
                    remote(
                        foreign(dy),
                        there,
                        cross_sem.at[0, s, way],
                        cross_sem.at[1, s, way],
                        device((1, -1)[way], 0),
                    ),
                )
            launch(
                key_of(0, dy),
                remote(there, there, cross_sem.at[0, s, 2], cross_sem.at[1, s, 2], device(2, 0)),
            )

        def cross_recv(dy, way):
            s = dy % SIDE
            ref = held[c].at[blk((-1, 1, 2)[way], dy)]
            remote(
                ref, ref, cross_sem.at[0, s, way], cross_sem.at[1, s, way], device(2, 0)
            ).wait_recv()

        done = {}

        def unit(cls, block, ends):
            depth = widths[cls] // 2

            def body(index, carry):
                gate, upper = carry
                low = pl.multiple_of(index * depth, depth)
                deep = pl.ds(pl.multiple_of(offsets[cls] + low, 128), depth)
                piece = held[cls][block, :, pl.ds(low, depth)]
                return (
                    gate + jnp.dot(piece, gate_ref[deep, :], preferred_element_type=F32),
                    upper + jnp.dot(piece, up_ref[deep, :], preferred_element_type=F32),
                )

            if ends:
                start = (total[block, :, 0:units], total[block, :, units : 2 * units])
            else:
                start = (jnp.zeros((rows, units), F32), jnp.zeros((rows, units), F32))
            gate, upper = lax.fori_loop(0, 2, body, start)
            if ends:
                hidden[block] = (jax.nn.silu(gate) * upper).astype(BF)
            else:
                total[block, :, 0:units] = gate
                total[block, :, units : 2 * units] = upper

        def compute(cls, places):
            if cls != c:
                for place in places:
                    chip_copy(cls, *place).wait_recv()
            for ends in (False, True):
                group = [p for p in places if (key_of(*p) in done) == ends]
                if not group:
                    continue

                def body(index, carry):
                    block = blk(*group[0])
                    for number in range(1, len(group)):
                        block = jnp.where(index == number, blk(*group[number]), block)
                    unit(cls, block, ends)
                    return carry

                if len(group) == 1:
                    body(0, 0)
                else:
                    lax.fori_loop(0, len(group), body, 0)
            for place in places:
                done[key_of(*place)] = True

        beside_y = [(0, -1), (0, 1)]
        if c == 0:
            cross_send(0)
            y_start(0)
            share(0, 0)
            swap_down()
            loaded(0)
            loaded(1)
            compute(0, [(0, 0)])
            compute(1, [(0, 0)])
            for way in range(2):
                y_full_recv(0, way)
                share(*beside_y[way])
            compute(0, beside_y)
            compute(1, beside_y)
            for way, dx in enumerate((-1, 1, 2)):
                cross_recv(0, way)
                y_start(dx % SIDE)
                share(dx, 0)
            compute(0, [(-1, 0), (1, 0), (2, 0)])
            y_half_recv(0)
            share(0, 2)
            compute(1, [(-1, 0), (1, 0), (2, 0)])
            compute(0, [(0, 2)])
            compute(1, [(0, 2)])
            for dx in (-1, 1, 2):
                for way in range(2):
                    y_full_recv(dx % SIDE, way)
                    share(dx, (-1, 1)[way])
                compute(0, [(dx, -1), (dx, 1)])
                if dx != 2:
                    compute(1, [(-1, dx), (1, dx), (2, dx)])
            for dx in (-1, 1):
                y_half_recv(dx % SIDE)
                share(dx, 2)
                compute(0, [(dx, 2)])
            y_half_recv(2)
            share(2, 2)
            compute(0, [(2, 2)])
            compute(1, [(-1, 2), (1, 2), (2, 2)])
        else:
            y_start(0)
            y_start(1)
            cross_send(0)
            share(0, 0)
            swap_down()
            loaded(0)
            loaded(1)
            compute(1, [(0, 0)])
            compute(0, [(0, 0)])
            for way in range(2):
                for op in range(2):
                    y_full_recv(op, way)
                cross_send((-1, 1)[way])
                share(*beside_y[way])
            compute(1, beside_y)
            compute(0, beside_y)
            for way, dx in enumerate((-1, 1, 2)):
                cross_recv(0, way)
                share(dx, 0)
            compute(1, [(-1, 0), (1, 0), (2, 0)])
            for op in range(2):
                y_half_recv(op)
            cross_send(2)
            share(0, 2)
            compute(0, [(-1, 0), (1, 0), (2, 0)])
            compute(1, [(0, 2)])
            compute(0, [(0, 2)])
            for dy in (-1, 1):
                for way, dx in enumerate((-1, 1, 2)):
                    cross_recv(dy, way)
                    share(dx, dy)
                compute(1, [(-1, dy), (1, dy), (2, dy)])
                compute(0, [(dy, -1), (dy, 1)])
            compute(0, [(2, -1), (2, 1)])
            compute(0, [(-1, 2), (1, 2)])
            for way, dx in enumerate((-1, 1, 2)):
                cross_recv(2, way)
                share(dx, 2)
            compute(1, [(-1, 2), (1, 2), (2, 2)])
            compute(0, [(2, 2)])

        loaded(2)
        step = 512

        def product(cls, block, dest, terms):
            span = widths[cls] // 2
            for part in range(2):

                def body(index, carry):
                    low = pl.multiple_of(index * step, 128)
                    here = pl.multiple_of(low + part * span, 128)
                    columns = pl.ds(here, step)
                    value = None
                    if block is not None:
                        value = jnp.dot(
                            hidden[block],
                            down_ref[:, pl.ds(pl.multiple_of(here + offsets[cls], 128), step)],
                            preferred_element_type=F32,
                        )
                    for get, which in terms:
                        if which is None:
                            term = get(columns).astype(F32)
                        elif which == part:
                            term = get(pl.ds(low, step)).astype(F32)
                        else:
                            continue
                        value = term if value is None else value + term
                    dest[:, columns] = value.astype(BF)
                    return carry

                lax.fori_loop(0, span // step, body, 0)

        orders = (
            [(2, 2), (1, 2), (-1, 2), (0, 2), (2, 1), (2, -1), (1, 1), (1, -1), (2, 0)]
            + [(-1, 1), (-1, -1), (1, 0), (0, 1), (0, -1), (-1, 0), (0, 0)],
            [(2, 2), (1, 2), (-1, 2), (2, 1), (1, 1), (-1, 1), (0, 2), (2, -1), (1, -1)]
            + [(-1, -1), (0, 1), (2, 0), (1, 0), (-1, 0), (0, -1), (0, 0)],
        )
        queue = list(orders[1 - c])

        def inner_copy(cls, dx, dy):
            i = dx % SIDE * SIDE + dy % SIDE
            return remote(
                held[cls].at[blk(dx, dy)],
                inner.at[blk(dx, dy), :, pl.ds(0, widths[cls])],
                r_chip_sem.at[0, i],
                r_chip_sem.at[1, i],
                sibling,
            )

        def feed():
            if queue:
                dx, dy = queue.pop(0)
                block = blk(dx, dy)
                product(1 - c, block, held[1 - c].at[block], ())
                launch(("chip", dx, dy), inner_copy(1 - c, dx, dy))

        served = []

        def chip_sum(dx, dy, terms):
            served.append((dx, dy))
            block = blk(dx, dy)
            inner_copy(c, dx, dy).wait_recv()
            settle(key_of(dx, dy))
            product(
                c,
                block,
                held[c].at[block],
                [(lambda columns: inner[block, :, columns], None)] + terms,
            )
            feed()

        def ring_back(op, way, ref, is_half):
            if is_half:
                return remote(
                    ref.at[:, pl.ds(way * half, half)],
                    r_half.at[op, way, :, pl.ds(0, half)],
                    r_ring_sem.at[0, op, way],
                    r_ring_sem.at[1, op, way],
                    device(0, (1, -1)[way]),
                )
            return remote(
                ref,
                r_full.at[op, way, :, pl.ds(0, width)],
                r_ring_sem.at[0, op, 2 + way],
                r_ring_sem.at[1, op, 2 + way],
                device(0, (1, -1)[way]),
            )

        def half_term(op, way):
            ring_back(op, way, held[c].at[0], True).wait_recv()
            return (lambda columns: r_half[op, way, :, columns], way)

        def full_terms(op):
            for way in range(2):
                ring_back(op, way, held[c].at[0], False).wait_recv()
            return [
                (lambda columns: r_full[op, 0, :, columns], None),
                (lambda columns: r_full[op, 1, :, columns], None),
            ]

        def crossed(s, way):
            return x_recv0.at[way] if c == 0 else x_recv1.at[s, way]

        def cross_back(s, way, ref):
            return remote(
                ref,
                crossed(s, way),
                r_cross_sem.at[0, s, way],
                r_cross_sem.at[1, s, way],
                device((1, -1, 2)[way], 0),
            )

        def cross_term(s, way):
            cross_back(s, way, held[c].at[0]).wait_recv()
            return (lambda columns: crossed(s, way)[:, columns], None)

        ours, theirs = held[c].at[blk(0, 0)], foreign(0)
        feed()
        feed()
        if c == 0:

            def far(dx):
                chip_sum(dx, 2, [])
                for way in range(2):
                    launch("back", ring_back(dx % SIDE, way, held0.at[blk(dx, 2)], True))

            def near(dx):
                for way in range(2):
                    dy = (1, -1)[way]
                    chip_sum(dx, dy, [half_term(dx % SIDE, way)])
                    launch("back", ring_back(dx % SIDE, way, held0.at[blk(dx, dy)], False))

            def home(dx):
                terms = full_terms(dx % SIDE)
                if dx == 0:
                    terms.append(cross_term(0, 2))
                chip_sum(dx, 0, terms)
                if dx != 0:
                    way = {1: 0, -1: 1, 2: 2}[dx]
                    launch("back", cross_back(0, way, held0.at[blk(dx, 0)]))

            for dx in (2, 1, -1, 0):
                far(dx)
            near(2)
            near(1)
            home(2)
            near(-1)
            home(1)
            near(0)
            home(-1)
            home(0)
            settle(("F", 0))
            product(0, None, theirs, [cross_term(0, 0), cross_term(0, 1)])
        else:

            def away(dy):
                for way, dx in ((2, 2), (0, 1), (1, -1)):
                    chip_sum(dx, dy, [])
                    launch("back", cross_back(dy % SIDE, way, held1.at[blk(dx, dy)]))

            def home(dy):
                s = dy % SIDE
                extra = ([], [])
                for op in range(2):
                    if dy in (1, -1):
                        extra[op].append(half_term(op, (1, -1).index(dy)))
                    if dy == 0:
                        extra[op].extend(full_terms(op))
                chip_sum(0, dy, [cross_term(s, 2)] + extra[0])
                settle(("F", s))
                other = foreign(dy)
                product(1, None, other, [cross_term(s, 0), cross_term(s, 1)] + extra[1])
                for op, ref in enumerate((held1.at[blk(0, dy)], other)):
                    if dy == 2:
                        for way in range(2):
                            launch("back", ring_back(op, way, ref, True))
                    elif dy != 0:
                        launch("back", ring_back(op, (1, -1).index(dy), ref, False))

            away(2)
            away(1)
            home(2)
            away(-1)
            home(1)
            away(0)
            home(-1)
            home(0)
        assert served == orders[c] and not queue

        here = pl.ds(offsets[c], width)
        there = pl.ds(offsets[1 - c], widths[1 - c])
        incoming = last.at[:, pl.ds(0, widths[1 - c])]

        def finish(keep, give):
            copy = remote(
                give, last.at[:, pl.ds(0, width)], last_sem.at[0], last_sem.at[1], sibling
            )
            copy.start()
            out_ref[:, here] = keep[...]
            remote(incoming, incoming, last_sem.at[0], last_sem.at[1], sibling).wait_recv()
            copy.wait_send()

        @pl.when(kind == c)
        def _():
            finish(ours, theirs)

        @pl.when(kind != c)
        def _():
            finish(theirs, ours)

        out_ref[:, there] = incoming[...]
        for key in list(pending):
            settle(key)

    for c in range(2):
        pl.when(core == c)(functools.partial(run, c))


def on_device(n_node, n_local):
    def run(
        patches,
        norm_gain,
        vit_up,
        vit_down,
        adapter,
        text_rows,
        router,
        expert_ids,
        w_gate,
        w_up,
        w_down,
    ):
        vmem = pl.BlockSpec(memory_space=pltpu.VMEM)
        hbm = pl.BlockSpec(memory_space=pl.ANY)
        row_count, model = expert_ids.shape[0], adapter.shape[1]
        experts = router.shape[1]
        capacity = 7 * row_count // (8 * n_node)
        rows, width = patches.shape
        lanes = 128 * ((width // n_local + 127) // 128)
        own_rows = n_node * capacity
        units = w_gate.shape[2]
        half = model // 2
        first = model * 3 // 5 // 512 * 512
        second = model - first
        swapped = [jax.ShapeDtypeStruct(w.shape[1:], BF) for w in (w_gate, w_up)]
        own, gate_swap, up_swap = pl.pallas_call(
            functools.partial(vision_kernel, n_node, n_local, capacity, first),
            out_shape=[jax.ShapeDtypeStruct((2, own_rows, first), BF)] + swapped,
            in_specs=[hbm, vmem, hbm, hbm, hbm, hbm, vmem, vmem] + [hbm] * 2,
            out_specs=[vmem] + [hbm] * 2,
            scratch_shapes=[
                pltpu.VMEM(patches.shape, BF),
                pltpu.VMEM(vit_up.shape[::-1], BF),
                pltpu.VMEM(vit_down.shape, BF),
                pltpu.VMEM(adapter.shape, BF),
                pltpu.VMEM(text_rows.shape, BF),
                pltpu.SemaphoreType.DMA((5,)),
                pltpu.VMEM((2, experts, PAD, first + row_count), BF),
                pltpu.VMEM((n_node, 2, PAD, first + row_count), BF),
                pltpu.VMEM((2, PAD, first // 2), BF),
                pltpu.VMEM((n_node, PAD, first // 2), BF),
                pltpu.VMEM((n_local, rows, lanes), BF),
                pltpu.VMEM((n_local, rows, lanes), BF),
                pltpu.VMEM((n_local, rows, lanes), BF),
                pltpu.VMEM((n_local, 2 * rows // n_local, half), BF),
                pltpu.VMEM((n_local, 2 * rows // n_local, half), BF),
                pltpu.SemaphoreType.DMA((4, n_local)),
                pltpu.SemaphoreType.DMA((4, n_node)),
                pltpu.SemaphoreType.DMA((2, 2, 8)),
            ],
            compiler_params=pltpu.CompilerParams(
                collective_id=0,
                has_side_effects=True,
                vmem_limit_bytes=63_000_000,
            ),
        )(
            patches,
            norm_gain.reshape(1, -1),
            vit_up.T,
            vit_down,
            adapter,
            text_rows,
            router.T,
            expert_ids.reshape(1, -1),
            w_gate,
            w_up,
        )
        result = pl.pallas_call(
            expert_kernel,
            out_shape=jax.ShapeDtypeStruct((own_rows, model), BF),
            in_specs=[hbm] * 6,
            out_specs=vmem,
            scratch_shapes=[
                pltpu.VMEM((model, units), BF),
                pltpu.VMEM((model, units), BF),
                pltpu.VMEM((units, model), BF),
                pltpu.VMEM((n_local, own_rows, first), BF),
                pltpu.VMEM((n_local, own_rows, second), BF),
                pltpu.VMEM((own_rows, first), BF),
                pltpu.VMEM((SIDE, own_rows, second), BF),
                pltpu.VMEM((n_local, own_rows, 2 * units), F32),
                pltpu.VMEM((n_local, own_rows, units), BF),
                pltpu.VMEM((n_local, own_rows, first), BF),
                pltpu.VMEM((SIDE, 2, own_rows, first // 2), BF),
                pltpu.VMEM((SIDE, 2, own_rows, first), BF),
                pltpu.VMEM((3, own_rows, first), BF),
                pltpu.VMEM((SIDE, 3, own_rows, second), BF),
                pltpu.VMEM((own_rows, first), BF),
                pltpu.SemaphoreType.DMA((5,)),
                pltpu.SemaphoreType.DMA((2, 2)),
                pltpu.SemaphoreType.DMA((2, SIDE, 4)),
                pltpu.SemaphoreType.DMA((2, SIDE, 3)),
                pltpu.SemaphoreType.DMA((2, n_local)),
                pltpu.SemaphoreType.DMA((2, SIDE, 4)),
                pltpu.SemaphoreType.DMA((2, SIDE, 3)),
                pltpu.SemaphoreType.DMA((2, n_local)),
                pltpu.SemaphoreType.DMA((2,)),
            ],
            compiler_params=pltpu.CompilerParams(
                collective_id=1,
                has_side_effects=True,
                vmem_limit_bytes=63_000_000,
            ),
        )(own, w_gate, w_up, w_down, gate_swap, up_swap)
        return result[None]

    return run


def solution(mesh):
    in_specs = (
        P("node", None),
        P(),
        P(None, "local"),
        P("local", None),
        P("local", None),
        P(("node", "local"), None),
        P(),
        P(("node", "local"), None),
        P("node", None, "local"),
        P("node", None, "local"),
        P("node", "local", None),
    )
    out_specs = P("node", "local", None)
    return jax.shard_map(
        on_device(mesh.shape["node"], mesh.shape["local"]),
        mesh=mesh,
        in_specs=in_specs,
        out_specs=out_specs,
        check_vma=False,
    )
```

```python
import functools

import jax
import jax.numpy as jnp
from jax import lax
from jax.experimental import pallas as pl
from jax.experimental.pallas import tpu as pltpu
from jax.sharding import PartitionSpec as P

MESH = pl.DeviceIdType.MESH
BF = jnp.bfloat16
F32 = jnp.float32
SIDE = 4
PAD = 16
SWAP = (1, 3, 5, 8)


def remote(src, dst, send_sem, recv_sem, device):
    return pltpu.make_async_remote_copy(
        src_ref=src,
        dst_ref=dst,
        send_sem=send_sem,
        recv_sem=recv_sem,
        device_id=device,
        device_id_type=MESH,
    )


def greet(devices):
    barrier = pltpu.get_barrier_semaphore()
    for device in devices:
        pl.semaphore_signal(barrier, inc=1, device_id=device, device_id_type=MESH)
    pl.semaphore_wait(barrier, len(devices))


def vision_kernel(
    n_node,
    n_local,
    capacity,
    share,
    patches_hbm,
    gain_ref,
    vit_up_hbm,
    vit_down_hbm,
    adapter_hbm,
    text_hbm,
    router_ref,
    ids_ref,
    gate_hbm,
    up_hbm,
    out_ref,
    gate_swap,
    up_swap,
    patches_ref,
    up_ref,
    down_ref,
    adapter_ref,
    text_ref,
    load_sem,
    slots,
    arrived,
    image_send,
    image_recv,
    part_send,
    part_recv,
    patch_blocks,
    embed_send,
    embed_recv,
    embed_send2,
    embed_recv2,
    sems,
    node_sem,
    swap_sem,
):
    node, local = lax.axis_index("node"), lax.axis_index("local")
    peers = [(node, lax.rem(local + k, n_local)) for k in range(1, n_local)]
    core = lax.rem(node, 2)
    x, y = local // SIDE, lax.rem(local, SIDE)
    column = [(lax.rem(node + k, n_node), local) for k in range(1, n_node)]
    sibling = node + 1 - 2 * core
    beside = [(sibling, lax.rem(x + d, SIDE) * SIDE + y) for d in (SIDE - 1, 1)]
    loads = [
        pltpu.make_async_copy(source, ref, load_sem.at[index])
        for index, (source, ref) in enumerate(
            (
                (patches_hbm, patches_ref),
                (vit_up_hbm, up_ref),
                (vit_down_hbm, down_ref),
                (text_hbm, text_ref),
                (adapter_hbm, adapter_ref),
            )
        )
    ]
    for load in loads:
        load.start()
    barrier = pltpu.get_barrier_semaphore()
    for device in peers + column + beside:
        pl.semaphore_signal(barrier, inc=1, device_id=device, device_id_type=MESH)

    units, model = gate_hbm.shape[2], gate_hbm.shape[1]
    swaps = []
    for index, (here, there) in enumerate(((gate_hbm, gate_swap), (up_hbm, up_swap))):
        for quarter in range(4):
            deep = pl.ds(quarter * (model // 4), model // 4)
            for way in range(2):
                part = pl.ds(way * (units // 2), units // 2)
                swaps.append(
                    remote(
                        here.at[0, deep, part],
                        there.at[deep, part],
                        swap_sem.at[0, way, index * 4 + quarter],
                        swap_sem.at[1, way, index * 4 + quarter],
                        beside[way],
                    )
                )

    def swap(low, high):
        @pl.when(core != lax.rem(x, 2))
        def _():
            for copy in swaps[2 * low : 2 * high]:
                copy.start()

    rows, width = patches_ref.shape
    block = width // n_local
    loads[0].wait()
    values = patches_ref[...].astype(F32)
    center = jnp.mean(values, axis=-1, keepdims=True)
    spread = jnp.mean((values - center) ** 2, axis=-1, keepdims=True)
    normed = ((values - center) * lax.rsqrt(spread + 1e-05) * gain_ref[...].reshape(1, -1)).astype(BF)
    pl.semaphore_wait(barrier, len(peers + column + beside))
    swap(0, SWAP[0])
    last_dims = (((1,), (1,)), ((), ()))
    loads[1].wait()
    loads[2].wait()
    inner = jax.nn.gelu(
        lax.dot_general(normed, up_ref[...], last_dims, preferred_element_type=F32),
        approximate=True,
    ).astype(BF)
    partial_sum = jnp.dot(inner, down_ref[...], preferred_element_type=F32)
    for index in range(n_local):
        low = index * block
        part_send[index, :, 0:block] = partial_sum[:, low : low + block].astype(BF)

    first = []
    for k in range(1, n_local):
        copy = remote(
            part_send.at[peers[k - 1][1]],
            part_recv.at[k],
            sems.at[0, k],
            sems.at[1, k],
            peers[k - 1],
        )
        copy.start()
        first.append(copy)
    swap(SWAP[0], SWAP[1])

    for index in range(n_local):
        low = index * block
        patch_blocks[index, :, 0:block] = values[:, low : low + block].astype(BF)
    text_rows = text_ref.shape[0]
    all_rows = ids_ref.shape[1]
    experts = router_ref.shape[0]
    square = (all_rows, all_rows)
    chosen = jnp.transpose(jnp.broadcast_to(ids_ref[...].astype(F32), square))[:, 0:1]
    table = (
        chosen == lax.broadcasted_iota(jnp.int32, (all_rows, experts), 1).astype(F32)
    ).astype(F32)
    earlier = (
        lax.broadcasted_iota(jnp.int32, square, 0) > lax.broadcasted_iota(jnp.int32, square, 1)
    ).astype(BF)
    counts = jnp.dot(earlier, table.astype(BF), preferred_element_type=F32)
    rank = jnp.sum(counts * table, axis=1, keepdims=True)
    slot = jnp.where(rank < capacity, chosen * PAD + rank, -1.0).astype(jnp.int32)
    place = jnp.transpose(
        (slot == lax.broadcasted_iota(jnp.int32, (all_rows, experts * PAD), 1)).astype(F32)
    ).astype(BF)
    loads[3].wait()
    logits = lax.dot_general(
        text_ref[...], router_ref[...], last_dims, preferred_element_type=F32
    )
    score = jax.nn.sigmoid(jnp.sum(logits * table[0:text_rows], axis=1, keepdims=True))
    step = 512
    shares = (share, model - share)

    def place_text(part, index, carry):
        low = pl.multiple_of(index * step, step)
        columns = pl.ds(pl.multiple_of(part * share + low, step), step)
        scaled = text_ref[:, columns].astype(F32) * score
        scaled = jnp.concatenate(
            [scaled, jnp.zeros((all_rows - text_rows, step), F32)], axis=0
        ).astype(BF)
        sent = jnp.dot(place, scaled, preferred_element_type=F32).astype(BF)
        for expert in range(experts):
            slots[part, expert, :, pl.ds(low, step)] = sent[expert * PAD : (expert + 1) * PAD]
        return carry

    for part in range(2):
        lax.fori_loop(0, shares[part] // step, functools.partial(place_text, part), 0)
        for expert in range(experts):
            slots[part, expert, :, share : share + all_rows] = place[
                expert * PAD : (expert + 1) * PAD
            ]

    def to_column(source_of, there, sem):
        copies = []
        for k in range(1, n_node):
            copy = remote(
                source_of(column[k - 1][0]),
                there.at[node],
                node_sem.at[sem, k],
                node_sem.at[sem + 1, k],
                column[k - 1],
            )
            copy.start()
            copies.append(copy)
        mine = pltpu.make_async_copy(source_of(node), there.at[node], node_sem.at[sem, 0])
        mine.start()

        def arrive():
            for k in range(1, n_node):
                source = there.at[lax.rem(node + n_node - k, n_node)]
                remote(
                    source, source, node_sem.at[sem, k], node_sem.at[sem + 1, k], column[k - 1]
                ).wait_recv()
            mine.wait()

        return copies, arrive

    third, text_arrives = to_column(
        lambda target: slots.at[lax.rem(target, 2), pl.ds(target // 2 * 2, 2)], arrived, 0
    )

    total = part_send[local, :, 0:block].astype(F32)
    for k in range(1, n_local):
        first[k - 1].wait_recv()
        total = total + part_recv[k, :, 0:block].astype(F32)
    vision = (patch_blocks[local, :, 0:block].astype(F32) + total).astype(BF)

    half = model // 2
    own = rows // n_local
    wide = 640

    loads[4].wait()

    def embed_part(index, carry):
        low = pl.ds(pl.multiple_of(index * wide, 128), wide)
        high = pl.ds(pl.multiple_of(index * wide + half, 128), wide)
        left = jnp.dot(vision, adapter_ref[:, low], preferred_element_type=F32)
        right = jnp.dot(vision, adapter_ref[:, high], preferred_element_type=F32)
        for j in range(n_local):
            spot = jnp.where(core == 0, j, j % SIDE * SIDE + j // SIDE)
            embed_send[spot, :, low] = jnp.concatenate(
                [left[j * own : (j + 1) * own], right[j * own : (j + 1) * own]], axis=0
            ).astype(BF)
        return carry

    lax.fori_loop(0, half // wide, embed_part, 0)

    p1, p2 = jnp.where(core == 0, x, y), jnp.where(core == 0, y, x)
    s1, s2 = jnp.where(core == 0, SIDE, 1), jnp.where(core == 0, 1, SIDE)
    second = []
    for d in range(1, SIDE):
        q1 = lax.rem(p1 + d, SIDE)
        copy = remote(
            embed_send.at[pl.ds(q1 * SIDE, SIDE)],
            embed_recv.at[d],
            sems.at[2, d],
            sems.at[3, d],
            (node, q1 * s1 + p2 * s2),
        )
        copy.start()
        second.append(copy)
    swap(SWAP[1], SWAP[2])
    for copy in second:
        copy.wait_recv()

    def ring_sum(q2):
        value = embed_send[p1 * SIDE + q2].astype(F32)
        for d in range(1, SIDE):
            value = value + embed_recv[d, q2].astype(F32)
        return value

    for d in range(1, SIDE):
        q2 = lax.rem(p2 + d, SIDE)
        embed_send2[d] = ring_sum(q2).astype(BF)
        copy = remote(
            embed_send2.at[d],
            embed_recv2.at[d],
            sems.at[2, SIDE + d],
            sems.at[3, SIDE + d],
            (node, p1 * s1 + q2 * s2),
        )
        copy.start()
        second.append(copy)
    swap(SWAP[2], SWAP[3])
    embed = ring_sum(p2)
    for d in range(1, SIDE):
        second[SIDE - 2 + d].wait_recv()
        embed = embed + embed_recv2[d].astype(F32)
    embed = embed.astype(BF).astype(F32)
    image = lax.dot_general(
        embed[0:own].astype(BF), router_ref[:, 0:half], last_dims, preferred_element_type=F32
    ) + lax.dot_general(
        embed[own : 2 * own].astype(BF),
        router_ref[:, half:model],
        last_dims,
        preferred_element_type=F32,
    )
    image_score = jax.nn.sigmoid(
        jnp.sum(image * table[text_rows:all_rows], axis=1, keepdims=True)
    )
    scaled = jnp.concatenate([embed[0:own], embed[own : 2 * own]], axis=1) * image_score
    for part in range(2):
        low, span = part * share, shares[part] // 2
        image_send[part, :, 0:span] = jnp.concatenate(
            [scaled[:, low : low + span], scaled[:, low + span : low + 2 * span]], axis=0
        ).astype(BF)
    fourth, image_arrives = to_column(
        lambda target: image_send.at[lax.rem(target, 2)], image_recv, 2
    )

    kept = out_ref.shape[1]
    wanted = lax.broadcasted_iota(jnp.int32, (kept, n_node * PAD), 0)
    origin = lax.broadcasted_iota(jnp.int32, (kept, n_node * PAD), 1)
    pick = (wanted // capacity * PAD + lax.rem(wanted, capacity) == origin).astype(BF)
    text_arrives()

    def compact(expert, index, carry):
        columns = pl.ds(pl.multiple_of(index * step, step), step)
        out_ref[expert, :, columns] = jnp.dot(
            pick,
            arrived[:, expert, :, columns].reshape(n_node * PAD, step),
            preferred_element_type=F32,
        ).astype(BF)
        return carry

    row = lax.broadcasted_iota(jnp.int32, (all_rows, n_node * PAD), 0)
    lane = lax.broadcasted_iota(jnp.int32, (all_rows, n_node * PAD), 1)
    same = (wanted // capacity == origin // PAD).astype(F32)
    spots = []
    for expert in range(2):
        lax.fori_loop(0, share // step, functools.partial(compact, expert), 0)
        places = jnp.dot(
            pick,
            arrived[:, expert, :, share : share + all_rows].reshape(n_node * PAD, all_rows),
            preferred_element_type=F32,
        ).astype(BF)
        for top in range(2):
            spread_rows = (
                (row - text_rows + top * own == lax.rem(lane, PAD)) & (row >= text_rows)
            ).astype(BF)
            spot = jnp.dot(places, spread_rows, preferred_element_type=F32) * same
            spots.append(spot.astype(BF))
    image_arrives()

    for c in range(2):

        @pl.when(core == c)
        def _(span=shares[c] // 2):
            for expert in range(2):
                for top in range(2):

                    def add(index, carry):
                        low = pl.multiple_of(index * step, step)
                        columns = pl.ds(pl.multiple_of(top * span + low, step), step)
                        image_rows = image_recv[:, :, pl.ds(low, step)]
                        out_ref[expert, :, columns] = (
                            out_ref[expert, :, columns].astype(F32)
                            + jnp.dot(
                                spots[2 * expert + top],
                                image_rows.reshape(n_node * PAD, step),
                                preferred_element_type=F32,
                            )
                        ).astype(BF)
                        return carry

                    lax.fori_loop(0, span // step, add, 0)

    for copy in first + second + third + fourth:
        copy.wait_send()

    @pl.when(core != lax.rem(x, 2))
    def _():
        for copy in swaps:
            copy.wait()


def wrap(p):
    return lax.rem(p + SIDE, SIDE)


def expert_kernel(
    own_ref,
    gate_hbm,
    up_hbm,
    down_hbm,
    gate_swap,
    up_swap,
    out_ref,
    gate_ref,
    up_ref,
    down_ref,
    held0,
    held1,
    foreign0,
    foreign1,
    total,
    hidden,
    inner,
    r_half,
    r_full,
    x_recv0,
    x_recv1,
    last,
    load_sem,
    swap_sem,
    ring_sem,
    cross_sem,
    chip_sem,
    r_ring_sem,
    r_cross_sem,
    r_chip_sem,
    last_sem,
):
    node, local = lax.axis_index("node"), lax.axis_index("local")
    core = lax.rem(node, 2)
    x, y = local // SIDE, lax.rem(local, SIDE)
    kind = lax.rem(x, 2)
    held = (held0, held1)
    widths = (held0.shape[2], held1.shape[2])
    offsets = (0, widths[0])
    rows = held0.shape[1]
    units = hidden.shape[2]
    sibling = (node + 1 - 2 * core, local)

    def device(dx, dy):
        return (node, wrap(x + dx) * SIDE + wrap(y + dy))

    def blk(dx, dy):
        return wrap(x + dx) * SIDE + wrap(y + dy)

    beside = [(sibling[0], device(d, 0)[1]) for d in (-1, 1)]
    greet(
        [sibling, device(1, 0), device(-1, 0), device(2, 0), device(0, 1), device(0, -1)] + beside
    )
    downs = [
        remote(
            down_hbm.at[0, pl.ds(way * (units // 2), units // 2), :],
            down_ref.at[pl.ds(way * (units // 2), units // 2), :],
            swap_sem.at[0, way],
            swap_sem.at[1, way],
            beside[way],
        )
        for way in range(2)
    ]
    own_down = pltpu.make_async_copy(down_hbm.at[0], down_ref, load_sem.at[2])

    @pl.when(core == kind)
    def _():
        for index, source in enumerate((gate_hbm, up_hbm)):
            ref = (gate_ref, up_ref)[index]
            pltpu.make_async_copy(source.at[0], ref, load_sem.at[index]).start()
        own_down.start()

    @pl.when(core != kind)
    def _():
        for index, source in enumerate((gate_swap, up_swap)):
            ref = (gate_ref, up_ref)[index]
            pltpu.make_async_copy(source, ref, load_sem.at[index]).start()

    def loaded(index):
        if index < 2:
            source, ref = ((gate_swap, gate_ref), (up_swap, up_ref))[index]
            pltpu.make_async_copy(source, ref, load_sem.at[index]).wait()
            return

        @pl.when(core == kind)
        def _():
            own_down.wait()

        @pl.when(core != kind)
        def _():
            for copy in downs:
                copy.wait()

    def swap_down():
        @pl.when(core != kind)
        def _():
            for copy in downs:
                copy.start()

    def run(c):
        pending = {}
        width = widths[c]
        half = width // 2

        def launch(key, copy):
            copy.start()
            pending.setdefault(key, []).append(copy)

        def settle(key):
            for copy in pending.pop(key, []):
                copy.wait_send()

        def key_of(dx, dy):
            return (dx % SIDE, dy % SIDE)

        def foreign(dy):
            return foreign0 if c == 0 else foreign1.at[wrap(y + dy)]

        pieces = [
            pltpu.make_async_copy(own_ref.at[index, :, pl.ds(0, width)], dest, load_sem.at[3 + n])
            for n, (index, dest) in enumerate(
                ((kind, held[c].at[blk(0, 0)]), (1 - kind, foreign(0)))
            )
        ]
        for piece in pieces:
            piece.start()
        for piece in pieces:
            piece.wait()

        def chip_copy(cls, dx, dy):
            ref = held[cls].at[blk(dx, dy)]
            i = dx % SIDE * SIDE + dy % SIDE
            return remote(ref, ref, chip_sem.at[0, i], chip_sem.at[1, i], sibling)

        def share(dx, dy):
            launch(key_of(dx, dy), chip_copy(c, dx, dy))

        def slot(op, dy, columns):
            if c == 0:
                return held0.at[blk(op, dy), :, columns], key_of(op, dy)
            if op == 0:
                return held1.at[blk(0, dy), :, columns], key_of(0, dy)
            return foreign1.at[wrap(y + dy), :, columns], ("F", dy % SIDE)

        def y_copy(op, way, dy, is_half):
            columns = pl.ds(way * half, half) if is_half else pl.ds(0, width)
            ref, key = slot(op, dy, columns)
            sem = 2 * is_half + way
            return key, remote(
                ref,
                ref,
                ring_sem.at[0, op, sem],
                ring_sem.at[1, op, sem],
                device(0, (1, -1)[way]),
            )

        def y_start(op):
            for way in range(2):
                launch(*y_copy(op, way, 0, False))

        def y_full_recv(op, way):
            dy = (-1, 1)[way]
            y_copy(op, way, dy, False)[1].wait_recv()
            launch(*y_copy(op, way, dy, True))

        def y_half_recv(op):
            for way in range(2):
                y_copy(op, way, 2, True)[1].wait_recv()

        def cross_send(dy):
            s = dy % SIDE
            there = held[c].at[blk(0, dy)]
            for way in range(2):
                launch(
                    ("F", s),
                    remote(
                        foreign(dy),
                        there,
                        cross_sem.at[0, s, way],
                        cross_sem.at[1, s, way],
                        device((1, -1)[way], 0),
                    ),
                )
            launch(
                key_of(0, dy),
                remote(there, there, cross_sem.at[0, s, 2], cross_sem.at[1, s, 2], device(2, 0)),
            )

        def cross_recv(dy, way):
            s = dy % SIDE
            ref = held[c].at[blk((-1, 1, 2)[way], dy)]
            remote(
                ref, ref, cross_sem.at[0, s, way], cross_sem.at[1, s, way], device(2, 0)
            ).wait_recv()

        done = {}

        def unit(cls, block, ends):
            depth = widths[cls] // 2

            def body(index, carry):
                gate, upper = carry
                low = pl.multiple_of(index * depth, depth)
                deep = pl.ds(pl.multiple_of(offsets[cls] + low, 128), depth)
                piece = held[cls][block, :, pl.ds(low, depth)]
                return (
                    gate + jnp.dot(piece, gate_ref[deep, :], preferred_element_type=F32),
                    upper + jnp.dot(piece, up_ref[deep, :], preferred_element_type=F32),
                )

            if ends:
                start = (total[block, :, 0:units], total[block, :, units : 2 * units])
            else:
                start = (jnp.zeros((rows, units), F32), jnp.zeros((rows, units), F32))
            gate, upper = lax.fori_loop(0, 2, body, start)
            if ends:
                hidden[block] = (jax.nn.silu(gate) * upper).astype(BF)
            else:
                total[block, :, 0:units] = gate
                total[block, :, units : 2 * units] = upper

        def compute(cls, places):
            if cls != c:
                for place in places:
                    chip_copy(cls, *place).wait_recv()
            for ends in (False, True):
                group = [p for p in places if (key_of(*p) in done) == ends]
                if not group:
                    continue

                def body(index, carry):
                    block = blk(*group[0])
                    for number in range(1, len(group)):
                        block = jnp.where(index == number, blk(*group[number]), block)
                    unit(cls, block, ends)
                    return carry

                if len(group) == 1:
                    body(0, 0)
                else:
                    lax.fori_loop(0, len(group), body, 0)
            for place in places:
                done[key_of(*place)] = True

        beside_y = [(0, -1), (0, 1)]
        if c == 0:
            cross_send(0)
            y_start(0)
            share(0, 0)
            loaded(0)
            loaded(1)
            compute(0, [(0, 0)])
            compute(1, [(0, 0)])
            for way in range(2):
                y_full_recv(0, way)
                share(*beside_y[way])
            compute(0, beside_y)
            compute(1, beside_y)
            for way, dx in enumerate((-1, 1, 2)):
                cross_recv(0, way)
                y_start(dx % SIDE)
                share(dx, 0)
            swap_down()
            compute(0, [(-1, 0), (1, 0), (2, 0)])
            y_half_recv(0)
            share(0, 2)
            compute(1, [(-1, 0), (1, 0), (2, 0)])
            compute(0, [(0, 2)])
            compute(1, [(0, 2)])
            for dx in (-1, 1, 2):
                for way in range(2):
                    y_full_recv(dx % SIDE, way)
                    share(dx, (-1, 1)[way])
                compute(0, [(dx, -1), (dx, 1)])
                if dx != 2:
                    compute(1, [(-1, dx), (1, dx), (2, dx)])
            for dx in (-1, 1):
                y_half_recv(dx % SIDE)
                share(dx, 2)
                compute(0, [(dx, 2)])
            y_half_recv(2)
            share(2, 2)
            compute(0, [(2, 2)])
            compute(1, [(-1, 2), (1, 2), (2, 2)])
        else:
            y_start(0)
            y_start(1)
            cross_send(0)
            share(0, 0)
            loaded(0)
            loaded(1)
            compute(1, [(0, 0)])
            compute(0, [(0, 0)])
            for way in range(2):
                for op in range(2):
                    y_full_recv(op, way)
                cross_send((-1, 1)[way])
                share(*beside_y[way])
            compute(1, beside_y)
            compute(0, beside_y)
            for way, dx in enumerate((-1, 1, 2)):
                cross_recv(0, way)
                share(dx, 0)
            compute(1, [(-1, 0), (1, 0), (2, 0)])
            for op in range(2):
                y_half_recv(op)
            cross_send(2)
            swap_down()
            share(0, 2)
            compute(0, [(-1, 0), (1, 0), (2, 0)])
            compute(1, [(0, 2)])
            compute(0, [(0, 2)])
            for dy in (-1, 1):
                for way, dx in enumerate((-1, 1, 2)):
                    cross_recv(dy, way)
                    share(dx, dy)
                compute(1, [(-1, dy), (1, dy), (2, dy)])
                compute(0, [(dy, -1), (dy, 1)])
            compute(0, [(2, -1), (2, 1)])
            compute(0, [(-1, 2), (1, 2)])
            for way, dx in enumerate((-1, 1, 2)):
                cross_recv(2, way)
                share(dx, 2)
            compute(1, [(-1, 2), (1, 2), (2, 2)])
            compute(0, [(2, 2)])

        loaded(2)
        step = 512

        def product(cls, block, dest, terms):
            span = widths[cls] // 2
            for part in range(2):

                def body(index, carry):
                    low = pl.multiple_of(index * step, 128)
                    here = pl.multiple_of(low + part * span, 128)
                    columns = pl.ds(here, step)
                    value = None
                    if block is not None:
                        value = jnp.dot(
                            hidden[block],
                            down_ref[:, pl.ds(pl.multiple_of(here + offsets[cls], 128), step)],
                            preferred_element_type=F32,
                        )
                    for get, which in terms:
                        if which is None:
                            term = get(columns).astype(F32)
                        elif which == part:
                            term = get(pl.ds(low, step)).astype(F32)
                        else:
                            continue
                        value = term if value is None else value + term
                    dest[:, columns] = value.astype(BF)
                    return carry

                lax.fori_loop(0, span // step, body, 0)

        orders = (
            [(2, 2), (1, 2), (-1, 2), (0, 2), (2, 1), (2, -1), (1, 1), (1, -1), (2, 0)]
            + [(-1, 1), (-1, -1), (1, 0), (0, 1), (0, -1), (-1, 0), (0, 0)],
            [(2, 2), (1, 2), (-1, 2), (2, 1), (1, 1), (-1, 1), (0, 2), (2, -1), (1, -1)]
            + [(-1, -1), (0, 1), (2, 0), (1, 0), (-1, 0), (0, -1), (0, 0)],
        )
        queue = list(orders[1 - c])

        def inner_copy(cls, dx, dy):
            i = dx % SIDE * SIDE + dy % SIDE
            return remote(
                held[cls].at[blk(dx, dy)],
                inner.at[blk(dx, dy), :, pl.ds(0, widths[cls])],
                r_chip_sem.at[0, i],
                r_chip_sem.at[1, i],
                sibling,
            )

        def feed():
            if queue:
                dx, dy = queue.pop(0)
                block = blk(dx, dy)
                product(1 - c, block, held[1 - c].at[block], ())
                launch(("chip", dx, dy), inner_copy(1 - c, dx, dy))

        served = []

        def chip_sum(dx, dy, terms):
            served.append((dx, dy))
            block = blk(dx, dy)
            inner_copy(c, dx, dy).wait_recv()
            settle(key_of(dx, dy))
            product(
                c,
                block,
                held[c].at[block],
                [(lambda columns: inner[block, :, columns], None)] + terms,
            )
            feed()

        def ring_back(op, way, ref, is_half):
            if is_half:
                return remote(
                    ref.at[:, pl.ds(way * half, half)],
                    r_half.at[op, way, :, pl.ds(0, half)],
                    r_ring_sem.at[0, op, way],
                    r_ring_sem.at[1, op, way],
                    device(0, (1, -1)[way]),
                )
            return remote(
                ref,
                r_full.at[op, way, :, pl.ds(0, width)],
                r_ring_sem.at[0, op, 2 + way],
                r_ring_sem.at[1, op, 2 + way],
                device(0, (1, -1)[way]),
            )

        def half_term(op, way):
            ring_back(op, way, held[c].at[0], True).wait_recv()
            return (lambda columns: r_half[op, way, :, columns], way)

        def full_terms(op):
            for way in range(2):
                ring_back(op, way, held[c].at[0], False).wait_recv()
            return [
                (lambda columns: r_full[op, 0, :, columns], None),
                (lambda columns: r_full[op, 1, :, columns], None),
            ]

        def crossed(s, way):
            return x_recv0.at[way] if c == 0 else x_recv1.at[s, way]

        def cross_back(s, way, ref):
            return remote(
                ref,
                crossed(s, way),
                r_cross_sem.at[0, s, way],
                r_cross_sem.at[1, s, way],
                device((1, -1, 2)[way], 0),
            )

        def cross_term(s, way):
            cross_back(s, way, held[c].at[0]).wait_recv()
            return (lambda columns: crossed(s, way)[:, columns], None)

        ours, theirs = held[c].at[blk(0, 0)], foreign(0)
        feed()
        feed()
        if c == 0:

            def far(dx):
                chip_sum(dx, 2, [])
                for way in range(2):
                    launch("back", ring_back(dx % SIDE, way, held0.at[blk(dx, 2)], True))

            def near(dx):
                for way in range(2):
                    dy = (1, -1)[way]
                    chip_sum(dx, dy, [half_term(dx % SIDE, way)])
                    launch("back", ring_back(dx % SIDE, way, held0.at[blk(dx, dy)], False))

            def home(dx):
                terms = full_terms(dx % SIDE)
                if dx == 0:
                    terms.append(cross_term(0, 2))
                chip_sum(dx, 0, terms)
                if dx != 0:
                    way = {1: 0, -1: 1, 2: 2}[dx]
                    launch("back", cross_back(0, way, held0.at[blk(dx, 0)]))

            for dx in (2, 1, -1, 0):
                far(dx)
            near(2)
            near(1)
            home(2)
            near(-1)
            home(1)
            near(0)
            home(-1)
            home(0)
            settle(("F", 0))
            product(0, None, theirs, [cross_term(0, 0), cross_term(0, 1)])
        else:

            def away(dy):
                for way, dx in ((2, 2), (0, 1), (1, -1)):
                    chip_sum(dx, dy, [])
                    launch("back", cross_back(dy % SIDE, way, held1.at[blk(dx, dy)]))

            def home(dy):
                s = dy % SIDE
                extra = ([], [])
                for op in range(2):
                    if dy in (1, -1):
                        extra[op].append(half_term(op, (1, -1).index(dy)))
                    if dy == 0:
                        extra[op].extend(full_terms(op))
                chip_sum(0, dy, [cross_term(s, 2)] + extra[0])
                settle(("F", s))
                other = foreign(dy)
                product(1, None, other, [cross_term(s, 0), cross_term(s, 1)] + extra[1])
                for op, ref in enumerate((held1.at[blk(0, dy)], other)):
                    if dy == 2:
                        for way in range(2):
                            launch("back", ring_back(op, way, ref, True))
                    elif dy != 0:
                        launch("back", ring_back(op, (1, -1).index(dy), ref, False))

            away(2)
            away(1)
            home(2)
            away(-1)
            home(1)
            away(0)
            home(-1)
            home(0)
        assert served == orders[c] and not queue

        here = pl.ds(offsets[c], width)
        there = pl.ds(offsets[1 - c], widths[1 - c])
        incoming = last.at[:, pl.ds(0, widths[1 - c])]

        def finish(keep, give):
            copy = remote(
                give, last.at[:, pl.ds(0, width)], last_sem.at[0], last_sem.at[1], sibling
            )
            copy.start()
            out_ref[:, here] = keep[...]
            remote(incoming, incoming, last_sem.at[0], last_sem.at[1], sibling).wait_recv()
            copy.wait_send()

        @pl.when(kind == c)
        def _():
            finish(ours, theirs)

        @pl.when(kind != c)
        def _():
            finish(theirs, ours)

        out_ref[:, there] = incoming[...]
        for key in list(pending):
            settle(key)

    for c in range(2):
        pl.when(core == c)(functools.partial(run, c))


def on_device(n_node, n_local):
    def run(
        patches,
        norm_gain,
        vit_up,
        vit_down,
        adapter,
        text_rows,
        router,
        expert_ids,
        w_gate,
        w_up,
        w_down,
    ):
        vmem = pl.BlockSpec(memory_space=pltpu.VMEM)
        hbm = pl.BlockSpec(memory_space=pl.ANY)
        row_count, model = expert_ids.shape[0], adapter.shape[1]
        experts = router.shape[1]
        capacity = 7 * row_count // (8 * n_node)
        rows, width = patches.shape
        lanes = 128 * ((width // n_local + 127) // 128)
        own_rows = n_node * capacity
        units = w_gate.shape[2]
        half = model // 2
        first = model * 3 // 5 // 512 * 512
        second = model - first
        swapped = [jax.ShapeDtypeStruct(w.shape[1:], BF) for w in (w_gate, w_up)]
        own, gate_swap, up_swap = pl.pallas_call(
            functools.partial(vision_kernel, n_node, n_local, capacity, first),
            out_shape=[jax.ShapeDtypeStruct((2, own_rows, first), BF)] + swapped,
            in_specs=[hbm, vmem, hbm, hbm, hbm, hbm, vmem, vmem] + [hbm] * 2,
            out_specs=[vmem] + [hbm] * 2,
            scratch_shapes=[
                pltpu.VMEM(patches.shape, BF),
                pltpu.VMEM(vit_up.shape[::-1], BF),
                pltpu.VMEM(vit_down.shape, BF),
                pltpu.VMEM(adapter.shape, BF),
                pltpu.VMEM(text_rows.shape, BF),
                pltpu.SemaphoreType.DMA((5,)),
                pltpu.VMEM((2, experts, PAD, first + row_count), BF),
                pltpu.VMEM((n_node, 2, PAD, first + row_count), BF),
                pltpu.VMEM((2, PAD, first // 2), BF),
                pltpu.VMEM((n_node, PAD, first // 2), BF),
                pltpu.VMEM((n_local, rows, lanes), BF),
                pltpu.VMEM((n_local, rows, lanes), BF),
                pltpu.VMEM((n_local, rows, lanes), BF),
                pltpu.VMEM((n_local, 2 * rows // n_local, half), BF),
                pltpu.VMEM((SIDE, SIDE, 2 * rows // n_local, half), BF),
                pltpu.VMEM((SIDE, 2 * rows // n_local, half), BF),
                pltpu.VMEM((SIDE, 2 * rows // n_local, half), BF),
                pltpu.SemaphoreType.DMA((4, n_local)),
                pltpu.SemaphoreType.DMA((4, n_node)),
                pltpu.SemaphoreType.DMA((2, 2, 8)),
            ],
            compiler_params=pltpu.CompilerParams(
                collective_id=0,
                has_side_effects=True,
                vmem_limit_bytes=63_000_000,
            ),
        )(
            patches,
            norm_gain,
            vit_up.T,
            vit_down,
            adapter,
            text_rows,
            router.T,
            expert_ids.reshape(1, -1),
            w_gate,
            w_up,
        )
        result = pl.pallas_call(
            expert_kernel,
            out_shape=jax.ShapeDtypeStruct((own_rows, model), BF),
            in_specs=[hbm] * 6,
            out_specs=vmem,
            scratch_shapes=[
                pltpu.VMEM((model, units), BF),
                pltpu.VMEM((model, units), BF),
                pltpu.VMEM((units, model), BF),
                pltpu.VMEM((n_local, own_rows, first), BF),
                pltpu.VMEM((n_local, own_rows, second), BF),
                pltpu.VMEM((own_rows, first), BF),
                pltpu.VMEM((SIDE, own_rows, second), BF),
                pltpu.VMEM((n_local, own_rows, 2 * units), F32),
                pltpu.VMEM((n_local, own_rows, units), BF),
                pltpu.VMEM((n_local, own_rows, first), BF),
                pltpu.VMEM((SIDE, 2, own_rows, first // 2), BF),
                pltpu.VMEM((SIDE, 2, own_rows, first), BF),
                pltpu.VMEM((3, own_rows, first), BF),
                pltpu.VMEM((SIDE, 3, own_rows, second), BF),
                pltpu.VMEM((own_rows, first), BF),
                pltpu.SemaphoreType.DMA((5,)),
                pltpu.SemaphoreType.DMA((2, 2)),
                pltpu.SemaphoreType.DMA((2, SIDE, 4)),
                pltpu.SemaphoreType.DMA((2, SIDE, 3)),
                pltpu.SemaphoreType.DMA((2, n_local)),
                pltpu.SemaphoreType.DMA((2, SIDE, 4)),
                pltpu.SemaphoreType.DMA((2, SIDE, 3)),
                pltpu.SemaphoreType.DMA((2, n_local)),
                pltpu.SemaphoreType.DMA((2,)),
            ],
            compiler_params=pltpu.CompilerParams(
                collective_id=1,
                has_side_effects=True,
                vmem_limit_bytes=63_000_000,
            ),
        )(own, w_gate, w_up, w_down, gate_swap, up_swap)
        return result[None]

    return run


def solution(mesh):
    in_specs = (
        P("node", None),
        P(),
        P(None, "local"),
        P("local", None),
        P("local", None),
        P(("node", "local"), None),
        P(),
        P(("node", "local"), None),
        P("node", None, "local"),
        P("node", None, "local"),
        P("node", "local", None),
    )
    out_specs = P("node", "local", None)
    return jax.shard_map(
        on_device(mesh.shape["node"], mesh.shape["local"]),
        mesh=mesh,
        in_specs=in_specs,
        out_specs=out_specs,
        check_vma=False,
    )
```

```python
import functools

import jax
import jax.numpy as jnp
from jax import lax
from jax.experimental import pallas as pl
from jax.experimental.pallas import tpu as pltpu
from jax.sharding import PartitionSpec as P

MESH = pl.DeviceIdType.MESH
BF = jnp.bfloat16
F32 = jnp.float32
SIDE = 4
PAD = 16
SWAP = (1, 3, 4, 8)


def remote(src, dst, send_sem, recv_sem, device):
    return pltpu.make_async_remote_copy(
        src_ref=src,
        dst_ref=dst,
        send_sem=send_sem,
        recv_sem=recv_sem,
        device_id=device,
        device_id_type=MESH,
    )


def greet(devices):
    barrier = pltpu.get_barrier_semaphore()
    for device in devices:
        pl.semaphore_signal(barrier, inc=1, device_id=device, device_id_type=MESH)
    pl.semaphore_wait(barrier, len(devices))


def vision_kernel(
    n_node,
    n_local,
    capacity,
    share,
    patches_hbm,
    gain_ref,
    vit_up_hbm,
    vit_down_hbm,
    adapter_hbm,
    text_hbm,
    router_ref,
    ids_ref,
    gate_hbm,
    up_hbm,
    out_ref,
    gate_swap,
    up_swap,
    patches_ref,
    up_ref,
    down_ref,
    adapter_ref,
    text_ref,
    load_sem,
    slots,
    arrived,
    image_send,
    image_recv,
    part_send,
    part_recv,
    patch_blocks,
    embed_send,
    embed_recv,
    embed_send2,
    embed_recv2,
    sems,
    node_sem,
    swap_sem,
):
    node, local = lax.axis_index("node"), lax.axis_index("local")
    peers = [(node, lax.rem(local + k, n_local)) for k in range(1, n_local)]
    core = lax.rem(node, 2)
    x, y = local // SIDE, lax.rem(local, SIDE)
    column = [(lax.rem(node + k, n_node), local) for k in range(1, n_node)]
    sibling = node + 1 - 2 * core
    beside = [(sibling, lax.rem(x + d, SIDE) * SIDE + y) for d in (SIDE - 1, 1)]
    loads = [
        pltpu.make_async_copy(source, ref, load_sem.at[index])
        for index, (source, ref) in enumerate(
            (
                (patches_hbm, patches_ref),
                (vit_up_hbm, up_ref),
                (vit_down_hbm, down_ref),
                (text_hbm, text_ref),
                (adapter_hbm, adapter_ref),
            )
        )
    ]
    for load in loads:
        load.start()
    barrier = pltpu.get_barrier_semaphore()
    for device in peers + column + beside:
        pl.semaphore_signal(barrier, inc=1, device_id=device, device_id_type=MESH)

    units, model = gate_hbm.shape[2], gate_hbm.shape[1]
    swaps = []
    for index, (here, there) in enumerate(((gate_hbm, gate_swap), (up_hbm, up_swap))):
        for quarter in range(4):
            deep = pl.ds(quarter * (model // 4), model // 4)
            for way in range(2):
                part = pl.ds(way * (units // 2), units // 2)
                swaps.append(
                    remote(
                        here.at[0, deep, part],
                        there.at[deep, part],
                        swap_sem.at[0, way, index * 4 + quarter],
                        swap_sem.at[1, way, index * 4 + quarter],
                        beside[way],
                    )
                )

    def swap(low, high):
        @pl.when(core != lax.rem(x, 2))
        def _():
            for copy in swaps[2 * low : 2 * high]:
                copy.start()

    rows, width = patches_ref.shape
    block = width // n_local
    loads[0].wait()
    values = patches_ref[...].astype(F32)
    center = jnp.mean(values, axis=-1, keepdims=True)
    spread = jnp.mean((values - center) ** 2, axis=-1, keepdims=True)
    normed = ((values - center) * lax.rsqrt(spread + 1e-05) * gain_ref[...].reshape(1, -1)).astype(BF)
    pl.semaphore_wait(barrier, len(peers + column + beside))
    swap(0, SWAP[0])
    last_dims = (((1,), (1,)), ((), ()))
    loads[1].wait()
    loads[2].wait()
    inner = jax.nn.gelu(
        lax.dot_general(normed, up_ref[...], last_dims, preferred_element_type=F32),
        approximate=True,
    ).astype(BF)
    partial_sum = jnp.dot(inner, down_ref[...], preferred_element_type=F32)
    for index in range(n_local):
        low = index * block
        part_send[index, :, 0:block] = partial_sum[:, low : low + block].astype(BF)

    first = []
    for k in range(1, n_local):
        copy = remote(
            part_send.at[peers[k - 1][1]],
            part_recv.at[k],
            sems.at[0, k],
            sems.at[1, k],
            peers[k - 1],
        )
        copy.start()
        first.append(copy)
    swap(SWAP[0], SWAP[1])

    for index in range(n_local):
        low = index * block
        patch_blocks[index, :, 0:block] = values[:, low : low + block].astype(BF)
    text_rows = text_ref.shape[0]
    all_rows = ids_ref.shape[1]
    experts = router_ref.shape[0]
    square = (all_rows, all_rows)
    chosen = jnp.transpose(jnp.broadcast_to(ids_ref[...].astype(F32), square))[:, 0:1]
    table = (
        chosen == lax.broadcasted_iota(jnp.int32, (all_rows, experts), 1).astype(F32)
    ).astype(F32)
    earlier = (
        lax.broadcasted_iota(jnp.int32, square, 0) > lax.broadcasted_iota(jnp.int32, square, 1)
    ).astype(BF)
    counts = jnp.dot(earlier, table.astype(BF), preferred_element_type=F32)
    rank = jnp.sum(counts * table, axis=1, keepdims=True)
    slot = jnp.where(rank < capacity, chosen * PAD + rank, -1.0).astype(jnp.int32)
    place = jnp.transpose(
        (slot == lax.broadcasted_iota(jnp.int32, (all_rows, experts * PAD), 1)).astype(F32)
    ).astype(BF)
    loads[3].wait()
    logits = lax.dot_general(
        text_ref[...], router_ref[...], last_dims, preferred_element_type=F32
    )
    score = jax.nn.sigmoid(jnp.sum(logits * table[0:text_rows], axis=1, keepdims=True))
    step = 512
    shares = (share, model - share)

    def place_text(part, index, carry):
        low = pl.multiple_of(index * step, step)
        columns = pl.ds(pl.multiple_of(part * share + low, step), step)
        scaled = text_ref[:, columns].astype(F32) * score
        scaled = jnp.concatenate(
            [scaled, jnp.zeros((all_rows - text_rows, step), F32)], axis=0
        ).astype(BF)
        sent = jnp.dot(place, scaled, preferred_element_type=F32).astype(BF)
        for expert in range(experts):
            slots[part, expert, :, pl.ds(low, step)] = sent[expert * PAD : (expert + 1) * PAD]
        return carry

    for part in range(2):
        lax.fori_loop(0, shares[part] // step, functools.partial(place_text, part), 0)
        for expert in range(experts):
            slots[part, expert, :, shares[part] : shares[part] + all_rows] = place[
                expert * PAD : (expert + 1) * PAD
            ]

    def to_column(source_of, there_of, sem):
        def each(step_of):
            for c in range(2):
                pl.when(core == c)(functools.partial(step_of, c))

        def copy_of(c, k):
            cls = c if k % 2 == 0 else 1 - c
            return remote(
                source_of(cls, column[k - 1][0]),
                there_of(cls, node),
                node_sem.at[sem, k],
                node_sem.at[sem + 1, k],
                column[k - 1],
            )

        def mine(c):
            return pltpu.make_async_copy(
                source_of(c, node), there_of(c, node), node_sem.at[sem, 0]
            )

        def begin(c):
            for k in range(1, n_node):
                copy_of(c, k).start()
            mine(c).start()

        def arrive(c):
            for k in range(1, n_node):
                source = there_of(c, lax.rem(node + n_node - k, n_node))
                remote(
                    source, source, node_sem.at[sem, k], node_sem.at[sem + 1, k], column[k - 1]
                ).wait_recv()
            mine(c).wait()

        def end(c):
            for k in range(1, n_node):
                copy_of(c, k).wait_send()

        each(begin)
        return functools.partial(each, arrive), functools.partial(each, end)

    def first_lanes(ref, cls, extra):
        return ref.at[:, :, pl.ds(0, shares[cls] + extra)]

    text_arrives, text_ends = to_column(
        lambda cls, target: first_lanes(
            slots.at[cls, pl.ds(target // 2 * 2, 2)], cls, all_rows
        ),
        lambda cls, source: first_lanes(arrived.at[source], cls, all_rows),
        0,
    )

    total = part_send[local, :, 0:block].astype(F32)
    for k in range(1, n_local):
        first[k - 1].wait_recv()
        total = total + part_recv[k, :, 0:block].astype(F32)
    vision = (patch_blocks[local, :, 0:block].astype(F32) + total).astype(BF)

    half = model // 2
    own = rows // n_local
    wide = 640

    loads[4].wait()

    def embed_part(index, carry):
        low = pl.ds(pl.multiple_of(index * wide, 128), wide)
        high = pl.ds(pl.multiple_of(index * wide + half, 128), wide)
        left = jnp.dot(vision, adapter_ref[:, low], preferred_element_type=F32)
        right = jnp.dot(vision, adapter_ref[:, high], preferred_element_type=F32)
        for j in range(n_local):
            spot = jnp.where(core == 0, j, j % SIDE * SIDE + j // SIDE)
            embed_send[spot, :, low] = jnp.concatenate(
                [left[j * own : (j + 1) * own], right[j * own : (j + 1) * own]], axis=0
            ).astype(BF)
        return carry

    lax.fori_loop(0, half // wide, embed_part, 0)

    p1, p2 = jnp.where(core == 0, x, y), jnp.where(core == 0, y, x)
    s1, s2 = jnp.where(core == 0, SIDE, 1), jnp.where(core == 0, 1, SIDE)
    second = []
    for d in range(1, SIDE):
        q1 = lax.rem(p1 + d, SIDE)
        copy = remote(
            embed_send.at[pl.ds(q1 * SIDE, SIDE)],
            embed_recv.at[d],
            sems.at[2, d],
            sems.at[3, d],
            (node, q1 * s1 + p2 * s2),
        )
        copy.start()
        second.append(copy)
    swap(SWAP[1], SWAP[2])
    for copy in second:
        copy.wait_recv()

    def ring_sum(q2):
        value = embed_send[p1 * SIDE + q2].astype(F32)
        for d in range(1, SIDE):
            value = value + embed_recv[d, q2].astype(F32)
        return value

    for d in range(1, SIDE):
        q2 = lax.rem(p2 + d, SIDE)
        embed_send2[d] = ring_sum(q2).astype(BF)
        copy = remote(
            embed_send2.at[d],
            embed_recv2.at[d],
            sems.at[2, SIDE + d],
            sems.at[3, SIDE + d],
            (node, p1 * s1 + q2 * s2),
        )
        copy.start()
        second.append(copy)
    swap(SWAP[2], SWAP[3])
    embed = ring_sum(p2)
    for d in range(1, SIDE):
        second[SIDE - 2 + d].wait_recv()
        embed = embed + embed_recv2[d].astype(F32)
    embed = embed.astype(BF).astype(F32)
    image = lax.dot_general(
        embed[0:own].astype(BF), router_ref[:, 0:half], last_dims, preferred_element_type=F32
    ) + lax.dot_general(
        embed[own : 2 * own].astype(BF),
        router_ref[:, half:model],
        last_dims,
        preferred_element_type=F32,
    )
    image_score = jax.nn.sigmoid(
        jnp.sum(image * table[text_rows:all_rows], axis=1, keepdims=True)
    )
    scaled = jnp.concatenate([embed[0:own], embed[own : 2 * own]], axis=1) * image_score
    for part in range(2):
        low, span = part * share, shares[part] // 2
        image_send[part, :, 0:span] = jnp.concatenate(
            [scaled[:, low : low + span], scaled[:, low + span : low + 2 * span]], axis=0
        ).astype(BF)
    image_arrives, image_ends = to_column(
        lambda cls, target: image_send.at[cls, :, pl.ds(0, shares[cls] // 2)],
        lambda cls, source: image_recv.at[source, :, pl.ds(0, shares[cls] // 2)],
        2,
    )

    kept = out_ref.shape[1]
    wanted = lax.broadcasted_iota(jnp.int32, (kept, n_node * PAD), 0)
    origin = lax.broadcasted_iota(jnp.int32, (kept, n_node * PAD), 1)
    pick = (wanted // capacity * PAD + lax.rem(wanted, capacity) == origin).astype(BF)
    text_arrives()

    def compact(expert, index, carry):
        columns = pl.ds(pl.multiple_of(index * step, step), step)
        out_ref[expert, :, columns] = jnp.dot(
            pick,
            arrived[:, expert, :, columns].reshape(n_node * PAD, step),
            preferred_element_type=F32,
        ).astype(BF)
        return carry

    row = lax.broadcasted_iota(jnp.int32, (all_rows, n_node * PAD), 0)
    lane = lax.broadcasted_iota(jnp.int32, (all_rows, n_node * PAD), 1)
    same = (wanted // capacity == origin // PAD).astype(F32)
    spots = []
    for expert in range(2):
        lax.fori_loop(0, share // step, functools.partial(compact, expert), 0)
        behind = pl.ds(pl.multiple_of(jnp.where(core == 0, shares[0], shares[1]), 128), all_rows)
        places = jnp.dot(
            pick,
            arrived[:, expert, :, behind].reshape(n_node * PAD, all_rows),
            preferred_element_type=F32,
        ).astype(BF)
        for top in range(2):
            spread_rows = (
                (row - text_rows + top * own == lax.rem(lane, PAD)) & (row >= text_rows)
            ).astype(BF)
            spot = jnp.dot(places, spread_rows, preferred_element_type=F32) * same
            spots.append(spot.astype(BF))
    image_arrives()

    for c in range(2):

        @pl.when(core == c)
        def _(span=shares[c] // 2):
            for expert in range(2):
                for top in range(2):

                    def add(index, carry):
                        low = pl.multiple_of(index * step, step)
                        columns = pl.ds(pl.multiple_of(top * span + low, step), step)
                        image_rows = image_recv[:, :, pl.ds(low, step)]
                        out_ref[expert, :, columns] = (
                            out_ref[expert, :, columns].astype(F32)
                            + jnp.dot(
                                spots[2 * expert + top],
                                image_rows.reshape(n_node * PAD, step),
                                preferred_element_type=F32,
                            )
                        ).astype(BF)
                        return carry

                    lax.fori_loop(0, span // step, add, 0)

    for copy in first + second:
        copy.wait_send()
    text_ends()
    image_ends()

    @pl.when(core != lax.rem(x, 2))
    def _():
        for copy in swaps:
            copy.wait()


def wrap(p):
    return lax.rem(p + SIDE, SIDE)


def expert_kernel(
    own_ref,
    gate_hbm,
    up_hbm,
    down_hbm,
    gate_swap,
    up_swap,
    out0_ref,
    out1_ref,
    gate_ref,
    up_ref,
    down_ref,
    held0,
    held1,
    foreign0,
    foreign1,
    total,
    hidden,
    inner,
    r_half,
    r_full,
    x_recv0,
    x_recv1,
    last,
    load_sem,
    swap_sem,
    ring_sem,
    cross_sem,
    chip_sem,
    r_ring_sem,
    r_cross_sem,
    r_chip_sem,
    last_sem,
):
    node, local = lax.axis_index("node"), lax.axis_index("local")
    core = lax.rem(node, 2)
    x, y = local // SIDE, lax.rem(local, SIDE)
    kind = lax.rem(x, 2)
    held = (held0, held1)
    widths = (held0.shape[2], held1.shape[2])
    offsets = (0, widths[0])
    rows = held0.shape[1]
    units = hidden.shape[2]
    sibling = (node + 1 - 2 * core, local)

    def device(dx, dy):
        return (node, wrap(x + dx) * SIDE + wrap(y + dy))

    def blk(dx, dy):
        return wrap(x + dx) * SIDE + wrap(y + dy)

    beside = [(sibling[0], device(d, 0)[1]) for d in (-1, 1)]
    downs = [
        remote(
            down_hbm.at[0, pl.ds(way * (units // 2), units // 2), :],
            down_ref.at[pl.ds(way * (units // 2), units // 2), :],
            swap_sem.at[0, way],
            swap_sem.at[1, way],
            beside[way],
        )
        for way in range(2)
    ]
    own_down = pltpu.make_async_copy(down_hbm.at[0], down_ref, load_sem.at[2])

    def own_pieces(c):
        places = (
            (kind, held[c].at[blk(0, 0)]),
            (1 - kind, foreign0 if c == 0 else foreign1.at[y]),
        )
        return [
            pltpu.make_async_copy(
                own_ref.at[index, :, pl.ds(0, widths[c])], dest, load_sem.at[3 + n]
            )
            for n, (index, dest) in enumerate(places)
        ]

    for c in range(2):

        @pl.when(core == c)
        def _():
            for piece in own_pieces(c):
                piece.start()

    @pl.when(core == kind)
    def _():
        for index, source in enumerate((gate_hbm, up_hbm)):
            ref = (gate_ref, up_ref)[index]
            pltpu.make_async_copy(source.at[0], ref, load_sem.at[index]).start()
        own_down.start()

    @pl.when(core != kind)
    def _():
        for index, source in enumerate((gate_swap, up_swap)):
            ref = (gate_ref, up_ref)[index]
            pltpu.make_async_copy(source, ref, load_sem.at[index]).start()

    greet(
        [sibling, device(1, 0), device(-1, 0), device(2, 0), device(0, 1), device(0, -1)] + beside
    )

    def loaded(index):
        if index < 2:
            source, ref = ((gate_swap, gate_ref), (up_swap, up_ref))[index]
            pltpu.make_async_copy(source, ref, load_sem.at[index]).wait()
            return

        @pl.when(core == kind)
        def _():
            own_down.wait()

        @pl.when(core != kind)
        def _():
            for copy in downs:
                copy.wait()

    def swap_down():
        @pl.when(core != kind)
        def _():
            for copy in downs:
                copy.start()

    def run(c):
        pending = {}
        width = widths[c]
        half = width // 2

        def launch(key, copy):
            copy.start()
            pending.setdefault(key, []).append(copy)

        def settle(key):
            for copy in pending.pop(key, []):
                copy.wait_send()

        def key_of(dx, dy):
            return (dx % SIDE, dy % SIDE)

        def foreign(dy):
            return foreign0 if c == 0 else foreign1.at[wrap(y + dy)]

        for piece in own_pieces(c):
            piece.wait()

        def chip_copy(cls, dx, dy):
            ref = held[cls].at[blk(dx, dy)]
            i = dx % SIDE * SIDE + dy % SIDE
            return remote(ref, ref, chip_sem.at[0, i], chip_sem.at[1, i], sibling)

        def share(dx, dy):
            launch(key_of(dx, dy), chip_copy(c, dx, dy))

        def slot(op, dy, columns):
            if c == 0:
                return held0.at[blk(op, dy), :, columns], key_of(op, dy)
            if op == 0:
                return held1.at[blk(0, dy), :, columns], key_of(0, dy)
            return foreign1.at[wrap(y + dy), :, columns], ("F", dy % SIDE)

        def y_copy(op, way, dy, is_half):
            columns = pl.ds(way * half, half) if is_half else pl.ds(0, width)
            ref, key = slot(op, dy, columns)
            sem = 2 * is_half + way
            return key, remote(
                ref,
                ref,
                ring_sem.at[0, op, sem],
                ring_sem.at[1, op, sem],
                device(0, (1, -1)[way]),
            )

        def y_start(op):
            for way in range(2):
                launch(*y_copy(op, way, 0, False))

        def y_full_recv(op, way):
            dy = (-1, 1)[way]
            y_copy(op, way, dy, False)[1].wait_recv()
            launch(*y_copy(op, way, dy, True))

        def y_half_recv(op):
            for way in range(2):
                y_copy(op, way, 2, True)[1].wait_recv()

        def cross_send(dy):
            s = dy % SIDE
            there = held[c].at[blk(0, dy)]
            for way in range(2):
                launch(
                    ("F", s),
                    remote(
                        foreign(dy),
                        there,
                        cross_sem.at[0, s, way],
                        cross_sem.at[1, s, way],
                        device((1, -1)[way], 0),
                    ),
                )
            launch(
                key_of(0, dy),
                remote(there, there, cross_sem.at[0, s, 2], cross_sem.at[1, s, 2], device(2, 0)),
            )

        def cross_recv(dy, way):
            s = dy % SIDE
            ref = held[c].at[blk((-1, 1, 2)[way], dy)]
            remote(
                ref, ref, cross_sem.at[0, s, way], cross_sem.at[1, s, way], device(2, 0)
            ).wait_recv()

        done = {}

        def unit(cls, block, ends):
            depth = widths[cls] // 2

            def body(index, carry):
                gate, upper = carry
                low = pl.multiple_of(index * depth, depth)
                deep = pl.ds(pl.multiple_of(offsets[cls] + low, 128), depth)
                piece = held[cls][block, :, pl.ds(low, depth)]
                return (
                    gate + jnp.dot(piece, gate_ref[deep, :], preferred_element_type=F32),
                    upper + jnp.dot(piece, up_ref[deep, :], preferred_element_type=F32),
                )

            if ends:
                start = (total[block, :, 0:units], total[block, :, units : 2 * units])
            else:
                start = (jnp.zeros((rows, units), F32), jnp.zeros((rows, units), F32))
            gate, upper = lax.fori_loop(0, 2, body, start)
            if ends:
                hidden[block] = (jax.nn.silu(gate) * upper).astype(BF)
            else:
                total[block, :, 0:units] = gate
                total[block, :, units : 2 * units] = upper

        def compute(cls, places):
            if cls != c:
                for place in places:
                    chip_copy(cls, *place).wait_recv()
            for ends in (False, True):
                group = [p for p in places if (key_of(*p) in done) == ends]
                if not group:
                    continue

                def body(index, carry):
                    block = blk(*group[0])
                    for number in range(1, len(group)):
                        block = jnp.where(index == number, blk(*group[number]), block)
                    unit(cls, block, ends)
                    return carry

                if len(group) == 1:
                    body(0, 0)
                else:
                    lax.fori_loop(0, len(group), body, 0)
            for place in places:
                done[key_of(*place)] = True

        beside_y = [(0, -1), (0, 1)]
        if c == 0:
            cross_send(0)
            y_start(0)
            share(0, 0)
            loaded(0)
            loaded(1)
            compute(0, [(0, 0)])
            compute(1, [(0, 0)])
            for way in range(2):
                y_full_recv(0, way)
                share(*beside_y[way])
            compute(0, beside_y)
            compute(1, beside_y)
            for way, dx in enumerate((-1, 1, 2)):
                cross_recv(0, way)
                y_start(dx % SIDE)
                share(dx, 0)
            swap_down()
            compute(0, [(-1, 0), (1, 0), (2, 0)])
            y_half_recv(0)
            share(0, 2)
            compute(1, [(-1, 0), (1, 0), (2, 0)])
            compute(0, [(0, 2)])
            compute(1, [(0, 2)])
            for dx in (-1, 1, 2):
                for way in range(2):
                    y_full_recv(dx % SIDE, way)
                    share(dx, (-1, 1)[way])
                compute(0, [(dx, -1), (dx, 1)])
                if dx != 2:
                    compute(1, [(-1, dx), (1, dx), (2, dx)])
            for dx in (-1, 1):
                y_half_recv(dx % SIDE)
                share(dx, 2)
                compute(0, [(dx, 2)])
            y_half_recv(2)
            share(2, 2)
            compute(0, [(2, 2)])
            compute(1, [(-1, 2), (1, 2), (2, 2)])
        else:
            y_start(0)
            y_start(1)
            cross_send(0)
            share(0, 0)
            loaded(0)
            loaded(1)
            compute(1, [(0, 0)])
            compute(0, [(0, 0)])
            for way in range(2):
                for op in range(2):
                    y_full_recv(op, way)
                cross_send((-1, 1)[way])
                share(*beside_y[way])
            compute(1, beside_y)
            compute(0, beside_y)
            for way, dx in enumerate((-1, 1, 2)):
                cross_recv(0, way)
                share(dx, 0)
            compute(1, [(-1, 0), (1, 0), (2, 0)])
            for op in range(2):
                y_half_recv(op)
            cross_send(2)
            swap_down()
            share(0, 2)
            compute(0, [(-1, 0), (1, 0), (2, 0)])
            compute(1, [(0, 2)])
            compute(0, [(0, 2)])
            for dy in (-1, 1):
                for way, dx in enumerate((-1, 1, 2)):
                    cross_recv(dy, way)
                    share(dx, dy)
                compute(1, [(-1, dy), (1, dy), (2, dy)])
                compute(0, [(dy, -1), (dy, 1)])
            compute(0, [(2, -1), (2, 1)])
            compute(0, [(-1, 2), (1, 2)])
            for way, dx in enumerate((-1, 1, 2)):
                cross_recv(2, way)
                share(dx, 2)
            compute(1, [(-1, 2), (1, 2), (2, 2)])
            compute(0, [(2, 2)])

        loaded(2)
        def product(cls, block, dest, terms):
            span = widths[cls] // 2
            step = span // 2
            for part in range(2):

                def body(index, carry):
                    low = pl.multiple_of(index * step, 128)
                    here = pl.multiple_of(low + part * span, 128)
                    columns = pl.ds(here, step)
                    value = None
                    if block is not None:
                        value = jnp.dot(
                            hidden[block],
                            down_ref[:, pl.ds(pl.multiple_of(here + offsets[cls], 128), step)],
                            preferred_element_type=F32,
                        )
                    for get, which in terms:
                        if which is None:
                            term = get(columns).astype(F32)
                        elif which == part:
                            term = get(pl.ds(low, step)).astype(F32)
                        else:
                            continue
                        value = term if value is None else value + term
                    dest[:, columns] = value.astype(BF)
                    return carry

                lax.fori_loop(0, span // step, body, 0)

        orders = (
            [(2, 2), (1, 2), (-1, 2), (0, 2), (2, 1), (2, -1), (1, 1), (1, -1), (2, 0)]
            + [(-1, 1), (-1, -1), (1, 0), (0, 1), (0, -1), (-1, 0), (0, 0)],
            [(2, 2), (1, 2), (-1, 2), (2, 1), (1, 1), (-1, 1), (0, 2), (2, -1), (1, -1)]
            + [(-1, -1), (0, 1), (2, 0), (1, 0), (-1, 0), (0, -1), (0, 0)],
        )
        queue = list(orders[1 - c])

        def inner_copy(cls, dx, dy):
            i = dx % SIDE * SIDE + dy % SIDE
            return remote(
                held[cls].at[blk(dx, dy)],
                inner.at[blk(dx, dy), :, pl.ds(0, widths[cls])],
                r_chip_sem.at[0, i],
                r_chip_sem.at[1, i],
                sibling,
            )

        def feed():
            if queue:
                dx, dy = queue.pop(0)
                block = blk(dx, dy)
                product(1 - c, block, held[1 - c].at[block], ())
                launch(("chip", dx, dy), inner_copy(1 - c, dx, dy))

        served = []

        def chip_sum(dx, dy, terms):
            served.append((dx, dy))
            block = blk(dx, dy)
            inner_copy(c, dx, dy).wait_recv()
            settle(key_of(dx, dy))
            product(
                c,
                block,
                held[c].at[block],
                [(lambda columns: inner[block, :, columns], None)] + terms,
            )
            feed()

        def ring_back(op, way, ref, is_half):
            if is_half:
                return remote(
                    ref.at[:, pl.ds(way * half, half)],
                    r_half.at[op, way, :, pl.ds(0, half)],
                    r_ring_sem.at[0, op, way],
                    r_ring_sem.at[1, op, way],
                    device(0, (1, -1)[way]),
                )
            return remote(
                ref,
                r_full.at[op, way, :, pl.ds(0, width)],
                r_ring_sem.at[0, op, 2 + way],
                r_ring_sem.at[1, op, 2 + way],
                device(0, (1, -1)[way]),
            )

        def half_term(op, way):
            ring_back(op, way, held[c].at[0], True).wait_recv()
            return (lambda columns: r_half[op, way, :, columns], way)

        def full_terms(op):
            for way in range(2):
                ring_back(op, way, held[c].at[0], False).wait_recv()
            return [
                (lambda columns: r_full[op, 0, :, columns], None),
                (lambda columns: r_full[op, 1, :, columns], None),
            ]

        def crossed(s, way):
            return x_recv0.at[way] if c == 0 else x_recv1.at[s, way]

        def cross_back(s, way, ref):
            return remote(
                ref,
                crossed(s, way),
                r_cross_sem.at[0, s, way],
                r_cross_sem.at[1, s, way],
                device((1, -1, 2)[way], 0),
            )

        def cross_term(s, way):
            cross_back(s, way, held[c].at[0]).wait_recv()
            return (lambda columns: crossed(s, way)[:, columns], None)

        ours, theirs = held[c].at[blk(0, 0)], foreign(0)
        feed()
        feed()
        if c == 0:

            def far(dx):
                chip_sum(dx, 2, [])
                for way in range(2):
                    launch("back", ring_back(dx % SIDE, way, held0.at[blk(dx, 2)], True))

            def near(dx):
                for way in range(2):
                    dy = (1, -1)[way]
                    chip_sum(dx, dy, [half_term(dx % SIDE, way)])
                    launch("back", ring_back(dx % SIDE, way, held0.at[blk(dx, dy)], False))

            def home(dx):
                terms = full_terms(dx % SIDE)
                if dx == 0:
                    terms.append(cross_term(0, 2))
                chip_sum(dx, 0, terms)
                if dx != 0:
                    way = {1: 0, -1: 1, 2: 2}[dx]
                    launch("back", cross_back(0, way, held0.at[blk(dx, 0)]))

            for dx in (2, 1, -1, 0):
                far(dx)
            near(2)
            near(1)
            home(2)
            near(-1)
            home(1)
            near(0)
            home(-1)
            home(0)
            settle(("F", 0))
            product(0, None, theirs, [cross_term(0, 0), cross_term(0, 1)])
        else:

            def away(dy):
                for way, dx in ((2, 2), (0, 1), (1, -1)):
                    chip_sum(dx, dy, [])
                    launch("back", cross_back(dy % SIDE, way, held1.at[blk(dx, dy)]))

            def home(dy):
                s = dy % SIDE
                extra = ([], [])
                for op in range(2):
                    if dy in (1, -1):
                        extra[op].append(half_term(op, (1, -1).index(dy)))
                    if dy == 0:
                        extra[op].extend(full_terms(op))
                chip_sum(0, dy, [cross_term(s, 2)] + extra[0])
                settle(("F", s))
                other = foreign(dy)
                product(1, None, other, [cross_term(s, 0), cross_term(s, 1)] + extra[1])
                for op, ref in enumerate((held1.at[blk(0, dy)], other)):
                    if dy == 2:
                        for way in range(2):
                            launch("back", ring_back(op, way, ref, True))
                    elif dy != 0:
                        launch("back", ring_back(op, (1, -1).index(dy), ref, False))

            away(2)
            away(1)
            home(2)
            away(-1)
            home(1)
            away(0)
            home(-1)
            home(0)
        assert served == orders[c] and not queue

        outs = (out0_ref, out1_ref)
        incoming = last.at[:, pl.ds(0, widths[1 - c])]

        def finish(keep, give):
            copy = remote(
                give, last.at[:, pl.ds(0, width)], last_sem.at[0], last_sem.at[1], sibling
            )
            copy.start()
            outs[c][...] = keep[...]
            remote(incoming, incoming, last_sem.at[0], last_sem.at[1], sibling).wait_recv()
            copy.wait_send()

        @pl.when(kind == c)
        def _():
            finish(ours, theirs)

        @pl.when(kind != c)
        def _():
            finish(theirs, ours)

        outs[1 - c][...] = incoming[...]
        for key in list(pending):
            settle(key)

    for c in range(2):
        pl.when(core == c)(functools.partial(run, c))


def on_device(n_node, n_local):
    def run(
        patches,
        norm_gain,
        vit_up,
        vit_down,
        adapter,
        text_rows,
        router,
        expert_ids,
        w_gate,
        w_up,
        w_down,
    ):
        vmem = pl.BlockSpec(memory_space=pltpu.VMEM)
        hbm = pl.BlockSpec(memory_space=pl.ANY)
        row_count, model = expert_ids.shape[0], adapter.shape[1]
        experts = router.shape[1]
        capacity = 7 * row_count // (8 * n_node)
        rows, width = patches.shape
        lanes = 128 * ((width // n_local + 127) // 128)
        own_rows = n_node * capacity
        units = w_gate.shape[2]
        half = model // 2
        first = model * 3 // 5 // 512 * 512
        second = model - first
        swapped = [jax.ShapeDtypeStruct(w.shape[1:], BF) for w in (w_gate, w_up)]
        own, gate_swap, up_swap = pl.pallas_call(
            functools.partial(vision_kernel, n_node, n_local, capacity, first),
            out_shape=[jax.ShapeDtypeStruct((2, own_rows, first), BF)] + swapped,
            in_specs=[hbm, vmem, hbm, hbm, hbm, hbm, vmem, vmem] + [hbm] * 2,
            out_specs=[vmem] + [hbm] * 2,
            scratch_shapes=[
                pltpu.VMEM(patches.shape, BF),
                pltpu.VMEM(vit_up.shape[::-1], BF),
                pltpu.VMEM(vit_down.shape, BF),
                pltpu.VMEM(adapter.shape, BF),
                pltpu.VMEM(text_rows.shape, BF),
                pltpu.SemaphoreType.DMA((5,)),
                pltpu.VMEM((2, experts, PAD, first + row_count), BF),
                pltpu.VMEM((n_node, 2, PAD, first + row_count), BF),
                pltpu.VMEM((2, PAD, first // 2), BF),
                pltpu.VMEM((n_node, PAD, first // 2), BF),
                pltpu.VMEM((n_local, rows, lanes), BF),
                pltpu.VMEM((n_local, rows, lanes), BF),
                pltpu.VMEM((n_local, rows, lanes), BF),
                pltpu.VMEM((n_local, 2 * rows // n_local, half), BF),
                pltpu.VMEM((SIDE, SIDE, 2 * rows // n_local, half), BF),
                pltpu.VMEM((SIDE, 2 * rows // n_local, half), BF),
                pltpu.VMEM((SIDE, 2 * rows // n_local, half), BF),
                pltpu.SemaphoreType.DMA((4, n_local)),
                pltpu.SemaphoreType.DMA((4, n_node)),
                pltpu.SemaphoreType.DMA((2, 2, 8)),
            ],
            compiler_params=pltpu.CompilerParams(
                collective_id=0,
                has_side_effects=True,
                vmem_limit_bytes=63_400_000,
            ),
        )(
            patches,
            norm_gain,
            vit_up.T,
            vit_down,
            adapter,
            text_rows,
            router.T,
            expert_ids.reshape(1, -1),
            w_gate,
            w_up,
        )
        result = pl.pallas_call(
            expert_kernel,
            out_shape=[jax.ShapeDtypeStruct((own_rows, size), BF) for size in (first, second)],
            in_specs=[hbm] * 6,
            out_specs=[vmem] * 2,
            scratch_shapes=[
                pltpu.VMEM((model, units), BF),
                pltpu.VMEM((model, units), BF),
                pltpu.VMEM((units, model), BF),
                pltpu.VMEM((n_local, own_rows, first), BF),
                pltpu.VMEM((n_local, own_rows, second), BF),
                pltpu.VMEM((own_rows, first), BF),
                pltpu.VMEM((SIDE, own_rows, second), BF),
                pltpu.VMEM((n_local, own_rows, 2 * units), F32),
                pltpu.VMEM((n_local, own_rows, units), BF),
                pltpu.VMEM((n_local, own_rows, first), BF),
                pltpu.VMEM((SIDE, 2, own_rows, first // 2), BF),
                pltpu.VMEM((SIDE, 2, own_rows, first), BF),
                pltpu.VMEM((3, own_rows, first), BF),
                pltpu.VMEM((SIDE, 3, own_rows, second), BF),
                pltpu.VMEM((own_rows, first), BF),
                pltpu.SemaphoreType.DMA((5,)),
                pltpu.SemaphoreType.DMA((2, 2)),
                pltpu.SemaphoreType.DMA((2, SIDE, 4)),
                pltpu.SemaphoreType.DMA((2, SIDE, 3)),
                pltpu.SemaphoreType.DMA((2, n_local)),
                pltpu.SemaphoreType.DMA((2, SIDE, 4)),
                pltpu.SemaphoreType.DMA((2, SIDE, 3)),
                pltpu.SemaphoreType.DMA((2, n_local)),
                pltpu.SemaphoreType.DMA((2,)),
            ],
            compiler_params=pltpu.CompilerParams(
                collective_id=1,
                has_side_effects=True,
                vmem_limit_bytes=63_400_000,
            ),
        )(own, w_gate, w_up, w_down, gate_swap, up_swap)
        return jnp.concatenate(result, axis=1)[None]

    return run


def solution(mesh):
    in_specs = (
        P("node", None),
        P(),
        P(None, "local"),
        P("local", None),
        P("local", None),
        P(("node", "local"), None),
        P(),
        P(("node", "local"), None),
        P("node", None, "local"),
        P("node", None, "local"),
        P("node", "local", None),
    )
    out_specs = P("node", "local", None)
    return jax.shard_map(
        on_device(mesh.shape["node"], mesh.shape["local"]),
        mesh=mesh,
        in_specs=in_specs,
        out_specs=out_specs,
        check_vma=False,
    )
```

```python
import functools

import jax
import jax.numpy as jnp
from jax import lax
from jax.experimental import pallas as pl
from jax.experimental.pallas import tpu as pltpu
from jax.sharding import PartitionSpec as P

MESH = pl.DeviceIdType.MESH
BF = jnp.bfloat16
F32 = jnp.float32
SIDE = 4
PAD = 16
SWAP = (1, 3, 4, 8)


def remote(src, dst, send_sem, recv_sem, device):
    return pltpu.make_async_remote_copy(
        src_ref=src,
        dst_ref=dst,
        send_sem=send_sem,
        recv_sem=recv_sem,
        device_id=device,
        device_id_type=MESH,
    )


def greet(devices):
    barrier = pltpu.get_barrier_semaphore()
    for device in devices:
        pl.semaphore_signal(barrier, inc=1, device_id=device, device_id_type=MESH)
    pl.semaphore_wait(barrier, len(devices))


def vision_kernel(
    n_node,
    n_local,
    capacity,
    share,
    patches_hbm,
    gain_ref,
    vit_up_hbm,
    vit_down_hbm,
    adapter_hbm,
    text_hbm,
    router_ref,
    ids_ref,
    gate_hbm,
    up_hbm,
    out_ref,
    gate_swap,
    up_swap,
    patches_ref,
    up_ref,
    down_ref,
    adapter_ref,
    text_ref,
    load_sem,
    slots,
    arrived,
    image_send,
    image_recv,
    part_send,
    part_recv,
    patch_blocks,
    embed_send,
    embed_recv,
    embed_send2,
    embed_recv2,
    sems,
    node_sem,
    swap_sem,
):
    node, local = lax.axis_index("node"), lax.axis_index("local")
    peers = [(node, lax.rem(local + k, n_local)) for k in range(1, n_local)]
    core = lax.rem(node, 2)
    x, y = local // SIDE, lax.rem(local, SIDE)
    column = [(lax.rem(node + k, n_node), local) for k in range(1, n_node)]
    sibling = node + 1 - 2 * core
    beside = [(sibling, lax.rem(x + d, SIDE) * SIDE + y) for d in (SIDE - 1, 1)]
    loads = [
        pltpu.make_async_copy(source, ref, load_sem.at[index])
        for index, (source, ref) in enumerate(
            (
                (patches_hbm, patches_ref),
                (vit_up_hbm, up_ref),
                (vit_down_hbm, down_ref),
                (text_hbm, text_ref),
                (adapter_hbm, adapter_ref),
            )
        )
    ]
    for load in loads:
        load.start()
    barrier = pltpu.get_barrier_semaphore()
    for device in peers + column + beside:
        pl.semaphore_signal(barrier, inc=1, device_id=device, device_id_type=MESH)

    units, model = gate_hbm.shape[2], gate_hbm.shape[1]
    swaps = []
    for index, (here, there) in enumerate(((gate_hbm, gate_swap), (up_hbm, up_swap))):
        for quarter in range(4):
            deep = pl.ds(quarter * (model // 4), model // 4)
            for way in range(2):
                part = pl.ds(way * (units // 2), units // 2)
                swaps.append(
                    remote(
                        here.at[0, deep, part],
                        there.at[deep, part],
                        swap_sem.at[0, way, index * 4 + quarter],
                        swap_sem.at[1, way, index * 4 + quarter],
                        beside[way],
                    )
                )

    def swap(low, high):
        @pl.when(core != lax.rem(x, 2))
        def _():
            for copy in swaps[2 * low : 2 * high]:
                copy.start()

    rows, width = patches_ref.shape
    block = width // n_local
    loads[0].wait()
    values = patches_ref[...].astype(F32)
    center = jnp.mean(values, axis=-1, keepdims=True)
    spread = jnp.mean((values - center) ** 2, axis=-1, keepdims=True)
    normed = ((values - center) * lax.rsqrt(spread + 1e-05) * gain_ref[...].reshape(1, -1)).astype(BF)
    pl.semaphore_wait(barrier, len(peers + column + beside))
    swap(0, SWAP[0])
    last_dims = (((1,), (1,)), ((), ()))
    loads[1].wait()
    loads[2].wait()
    inner = jax.nn.gelu(
        lax.dot_general(normed, up_ref[...], last_dims, preferred_element_type=F32),
        approximate=True,
    ).astype(BF)
    partial_sum = jnp.dot(inner, down_ref[...], preferred_element_type=F32)
    for index in range(n_local):
        low = index * block
        part_send[index, :, 0:block] = partial_sum[:, low : low + block].astype(BF)

    first = []
    for k in range(1, n_local):
        copy = remote(
            part_send.at[peers[k - 1][1]],
            part_recv.at[k],
            sems.at[0, k],
            sems.at[1, k],
            peers[k - 1],
        )
        copy.start()
        first.append(copy)
    swap(SWAP[0], SWAP[1])

    for index in range(n_local):
        low = index * block
        patch_blocks[index, :, 0:block] = values[:, low : low + block].astype(BF)
    text_rows = text_ref.shape[0]
    all_rows = ids_ref.shape[1]
    experts = router_ref.shape[0]
    square = (all_rows, all_rows)
    chosen = jnp.transpose(jnp.broadcast_to(ids_ref[...].astype(F32), square))[:, 0:1]
    table = (
        chosen == lax.broadcasted_iota(jnp.int32, (all_rows, experts), 1).astype(F32)
    ).astype(F32)
    earlier = (
        lax.broadcasted_iota(jnp.int32, square, 0) > lax.broadcasted_iota(jnp.int32, square, 1)
    ).astype(BF)
    counts = jnp.dot(earlier, table.astype(BF), preferred_element_type=F32)
    rank = jnp.sum(counts * table, axis=1, keepdims=True)
    slot = jnp.where(rank < capacity, chosen * PAD + rank, -1.0).astype(jnp.int32)
    place = jnp.transpose(
        (slot == lax.broadcasted_iota(jnp.int32, (all_rows, experts * PAD), 1)).astype(F32)
    ).astype(BF)
    loads[3].wait()
    logits = lax.dot_general(
        text_ref[...], router_ref[...], last_dims, preferred_element_type=F32
    )
    score = jax.nn.sigmoid(jnp.sum(logits * table[0:text_rows], axis=1, keepdims=True))
    step = 512
    shares = (share, model - share)

    def place_text(part, index, carry):
        low = pl.multiple_of(index * step, step)
        columns = pl.ds(pl.multiple_of(part * share + low, step), step)
        scaled = text_ref[:, columns].astype(F32) * score
        scaled = jnp.concatenate(
            [scaled, jnp.zeros((all_rows - text_rows, step), F32)], axis=0
        ).astype(BF)
        sent = jnp.dot(place, scaled, preferred_element_type=F32).astype(BF)
        for expert in range(experts):
            slots[part, expert, :, pl.ds(low, step)] = sent[expert * PAD : (expert + 1) * PAD]
        return carry

    for part in range(2):
        lax.fori_loop(0, shares[part] // step, functools.partial(place_text, part), 0)
        for expert in range(experts):
            slots[part, expert, :, shares[part] : shares[part] + all_rows] = place[
                expert * PAD : (expert + 1) * PAD
            ]

    def to_column(source_of, there_of, sem):
        def each(step_of):
            for c in range(2):
                pl.when(core == c)(functools.partial(step_of, c))

        def copy_of(c, k):
            cls = c if k % 2 == 0 else 1 - c
            return remote(
                source_of(cls, column[k - 1][0]),
                there_of(cls, node),
                node_sem.at[sem, k],
                node_sem.at[sem + 1, k],
                column[k - 1],
            )

        def mine(c):
            return pltpu.make_async_copy(
                source_of(c, node), there_of(c, node), node_sem.at[sem, 0]
            )

        def begin(c):
            for k in range(1, n_node):
                copy_of(c, k).start()
            mine(c).start()

        def arrive(c):
            for k in range(1, n_node):
                source = there_of(c, lax.rem(node + n_node - k, n_node))
                remote(
                    source, source, node_sem.at[sem, k], node_sem.at[sem + 1, k], column[k - 1]
                ).wait_recv()
            mine(c).wait()

        def end(c):
            for k in range(1, n_node):
                copy_of(c, k).wait_send()

        each(begin)
        return functools.partial(each, arrive), functools.partial(each, end)

    def first_lanes(ref, cls, extra):
        return ref.at[:, :, pl.ds(0, shares[cls] + extra)]

    text_arrives, text_ends = to_column(
        lambda cls, target: first_lanes(
            slots.at[cls, pl.ds(target // 2 * 2, 2)], cls, all_rows
        ),
        lambda cls, source: first_lanes(arrived.at[source], cls, all_rows),
        0,
    )

    total = part_send[local, :, 0:block].astype(F32)
    for k in range(1, n_local):
        first[k - 1].wait_recv()
        total = total + part_recv[k, :, 0:block].astype(F32)
    vision = (patch_blocks[local, :, 0:block].astype(F32) + total).astype(BF)

    half = model // 2
    own = rows // n_local
    wide = 640

    loads[4].wait()

    def embed_part(index, carry):
        low = pl.ds(pl.multiple_of(index * wide, 128), wide)
        high = pl.ds(pl.multiple_of(index * wide + half, 128), wide)
        left = jnp.dot(vision, adapter_ref[:, low], preferred_element_type=F32)
        right = jnp.dot(vision, adapter_ref[:, high], preferred_element_type=F32)
        for j in range(n_local):
            spot = jnp.where(core == 0, j, j % SIDE * SIDE + j // SIDE)
            embed_send[spot, :, low] = jnp.concatenate(
                [left[j * own : (j + 1) * own], right[j * own : (j + 1) * own]], axis=0
            ).astype(BF)
        return carry

    lax.fori_loop(0, half // wide, embed_part, 0)

    p1, p2 = jnp.where(core == 0, x, y), jnp.where(core == 0, y, x)
    s1, s2 = jnp.where(core == 0, SIDE, 1), jnp.where(core == 0, 1, SIDE)
    second = []
    for d in range(1, SIDE):
        q1 = lax.rem(p1 + d, SIDE)
        copy = remote(
            embed_send.at[pl.ds(q1 * SIDE, SIDE)],
            embed_recv.at[d],
            sems.at[2, d],
            sems.at[3, d],
            (node, q1 * s1 + p2 * s2),
        )
        copy.start()
        second.append(copy)
    swap(SWAP[1], SWAP[2])
    for copy in second:
        copy.wait_recv()

    def ring_sum(q2):
        value = embed_send[p1 * SIDE + q2].astype(F32)
        for d in range(1, SIDE):
            value = value + embed_recv[d, q2].astype(F32)
        return value

    for d in range(1, SIDE):
        q2 = lax.rem(p2 + d, SIDE)
        embed_send2[d] = ring_sum(q2).astype(BF)
        copy = remote(
            embed_send2.at[d],
            embed_recv2.at[d],
            sems.at[2, SIDE + d],
            sems.at[3, SIDE + d],
            (node, p1 * s1 + q2 * s2),
        )
        copy.start()
        second.append(copy)
    swap(SWAP[2], SWAP[3])
    embed = ring_sum(p2)
    for d in range(1, SIDE):
        second[SIDE - 2 + d].wait_recv()
        embed = embed + embed_recv2[d].astype(F32)
    embed = embed.astype(BF).astype(F32)
    image = lax.dot_general(
        embed[0:own].astype(BF), router_ref[:, 0:half], last_dims, preferred_element_type=F32
    ) + lax.dot_general(
        embed[own : 2 * own].astype(BF),
        router_ref[:, half:model],
        last_dims,
        preferred_element_type=F32,
    )
    image_score = jax.nn.sigmoid(
        jnp.sum(image * table[text_rows:all_rows], axis=1, keepdims=True)
    )
    scaled = jnp.concatenate([embed[0:own], embed[own : 2 * own]], axis=1) * image_score
    for part in range(2):
        low, span = part * share, shares[part] // 2
        image_send[part, :, 0:span] = jnp.concatenate(
            [scaled[:, low : low + span], scaled[:, low + span : low + 2 * span]], axis=0
        ).astype(BF)
    image_arrives, image_ends = to_column(
        lambda cls, target: image_send.at[cls, :, pl.ds(0, shares[cls] // 2)],
        lambda cls, source: image_recv.at[source, :, pl.ds(0, shares[cls] // 2)],
        2,
    )

    kept = out_ref.shape[1]
    wanted = lax.broadcasted_iota(jnp.int32, (kept, n_node * PAD), 0)
    origin = lax.broadcasted_iota(jnp.int32, (kept, n_node * PAD), 1)
    pick = (wanted // capacity * PAD + lax.rem(wanted, capacity) == origin).astype(BF)
    text_arrives()

    def compact(expert, index, carry):
        columns = pl.ds(pl.multiple_of(index * step, step), step)
        out_ref[expert, :, columns] = jnp.dot(
            pick,
            arrived[:, expert, :, columns].reshape(n_node * PAD, step),
            preferred_element_type=F32,
        ).astype(BF)
        return carry

    row = lax.broadcasted_iota(jnp.int32, (all_rows, n_node * PAD), 0)
    lane = lax.broadcasted_iota(jnp.int32, (all_rows, n_node * PAD), 1)
    same = (wanted // capacity == origin // PAD).astype(F32)
    spots = []
    for expert in range(2):
        lax.fori_loop(0, share // step, functools.partial(compact, expert), 0)
        behind = pl.ds(pl.multiple_of(jnp.where(core == 0, shares[0], shares[1]), 128), all_rows)
        places = jnp.dot(
            pick,
            arrived[:, expert, :, behind].reshape(n_node * PAD, all_rows),
            preferred_element_type=F32,
        ).astype(BF)
        for top in range(2):
            spread_rows = (
                (row - text_rows + top * own == lax.rem(lane, PAD)) & (row >= text_rows)
            ).astype(BF)
            spot = jnp.dot(places, spread_rows, preferred_element_type=F32) * same
            spots.append(spot.astype(BF))
    image_arrives()

    for c in range(2):

        @pl.when(core == c)
        def _(span=shares[c] // 2):
            for expert in range(2):
                for top in range(2):

                    def add(index, carry):
                        low = pl.multiple_of(index * step, step)
                        columns = pl.ds(pl.multiple_of(top * span + low, step), step)
                        image_rows = image_recv[:, :, pl.ds(low, step)]
                        out_ref[expert, :, columns] = (
                            out_ref[expert, :, columns].astype(F32)
                            + jnp.dot(
                                spots[2 * expert + top],
                                image_rows.reshape(n_node * PAD, step),
                                preferred_element_type=F32,
                            )
                        ).astype(BF)
                        return carry

                    lax.fori_loop(0, span // step, add, 0)

    for copy in first + second:
        copy.wait_send()
    text_ends()
    image_ends()

    @pl.when(core != lax.rem(x, 2))
    def _():
        for copy in swaps:
            copy.wait()


def wrap(p):
    return lax.rem(p + SIDE, SIDE)


def expert_kernel(
    own_ref,
    gate_hbm,
    up_hbm,
    down_hbm,
    gate_swap,
    up_swap,
    out0_ref,
    out1_ref,
    gate_ref,
    up_ref,
    down_ref,
    held0,
    held1,
    foreign0,
    foreign1,
    total,
    hidden,
    inner,
    r_half,
    r_full,
    x_recv0,
    x_recv1,
    last,
    load_sem,
    swap_sem,
    ring_sem,
    cross_sem,
    chip_sem,
    r_ring_sem,
    r_cross_sem,
    r_chip_sem,
    last_sem,
):
    node, local = lax.axis_index("node"), lax.axis_index("local")
    core = lax.rem(node, 2)
    x, y = local // SIDE, lax.rem(local, SIDE)
    kind = lax.rem(x, 2)
    held = (held0, held1)
    widths = (held0.shape[2], held1.shape[2])
    offsets = (0, widths[0])
    rows = held0.shape[1]
    units = hidden.shape[2]
    sibling = (node + 1 - 2 * core, local)

    def device(dx, dy):
        return (node, wrap(x + dx) * SIDE + wrap(y + dy))

    def blk(dx, dy):
        return wrap(x + dx) * SIDE + wrap(y + dy)

    beside = [(sibling[0], device(d, 0)[1]) for d in (-1, 1)]
    downs = [
        remote(
            down_hbm.at[0, pl.ds(way * (units // 2), units // 2), :],
            down_ref.at[pl.ds(way * (units // 2), units // 2), :],
            swap_sem.at[0, way],
            swap_sem.at[1, way],
            beside[way],
        )
        for way in range(2)
    ]
    own_down = pltpu.make_async_copy(down_hbm.at[0], down_ref, load_sem.at[2])

    def own_pieces(c):
        places = (
            (kind, held[c].at[blk(0, 0)]),
            (1 - kind, foreign0 if c == 0 else foreign1.at[y]),
        )
        return [
            pltpu.make_async_copy(
                own_ref.at[index, :, pl.ds(0, widths[c])], dest, load_sem.at[3 + n]
            )
            for n, (index, dest) in enumerate(places)
        ]

    for c in range(2):

        @pl.when(core == c)
        def _():
            for piece in own_pieces(c):
                piece.start()

    @pl.when(core == kind)
    def _():
        for index, source in enumerate((gate_hbm, up_hbm)):
            ref = (gate_ref, up_ref)[index]
            pltpu.make_async_copy(source.at[0], ref, load_sem.at[index]).start()
        own_down.start()

    @pl.when(core != kind)
    def _():
        for index, source in enumerate((gate_swap, up_swap)):
            ref = (gate_ref, up_ref)[index]
            pltpu.make_async_copy(source, ref, load_sem.at[index]).start()

    greet(
        [sibling, device(1, 0), device(-1, 0), device(2, 0), device(0, 1), device(0, -1)] + beside
    )

    def loaded(index):
        if index < 2:
            source, ref = ((gate_swap, gate_ref), (up_swap, up_ref))[index]
            pltpu.make_async_copy(source, ref, load_sem.at[index]).wait()
            return

        @pl.when(core == kind)
        def _():
            own_down.wait()

        @pl.when(core != kind)
        def _():
            for copy in downs:
                copy.wait()

    def swap_down():
        @pl.when(core != kind)
        def _():
            for copy in downs:
                copy.start()

    def run(c):
        pending = {}
        width = widths[c]
        half = width // 2

        def launch(key, copy):
            copy.start()
            pending.setdefault(key, []).append(copy)

        def settle(key):
            for copy in pending.pop(key, []):
                copy.wait_send()

        def key_of(dx, dy):
            return (dx % SIDE, dy % SIDE)

        def foreign(dy):
            return foreign0 if c == 0 else foreign1.at[wrap(y + dy)]

        for piece in own_pieces(c):
            piece.wait()

        def chip_copy(cls, dx, dy):
            ref = held[cls].at[blk(dx, dy)]
            i = dx % SIDE * SIDE + dy % SIDE
            return remote(ref, ref, chip_sem.at[0, i], chip_sem.at[1, i], sibling)

        def share(dx, dy):
            launch(key_of(dx, dy), chip_copy(c, dx, dy))

        def slot(op, dy, columns):
            if c == 0:
                return held0.at[blk(op, dy), :, columns], key_of(op, dy)
            if op == 0:
                return held1.at[blk(0, dy), :, columns], key_of(0, dy)
            return foreign1.at[wrap(y + dy), :, columns], ("F", dy % SIDE)

        def y_copy(op, way, dy, is_half):
            columns = pl.ds(way * half, half) if is_half else pl.ds(0, width)
            ref, key = slot(op, dy, columns)
            sem = 2 * is_half + way
            return key, remote(
                ref,
                ref,
                ring_sem.at[0, op, sem],
                ring_sem.at[1, op, sem],
                device(0, (1, -1)[way]),
            )

        def y_start(op):
            for way in range(2):
                launch(*y_copy(op, way, 0, False))

        def y_full_recv(op, way):
            dy = (-1, 1)[way]
            y_copy(op, way, dy, False)[1].wait_recv()
            launch(*y_copy(op, way, dy, True))

        def y_half_recv(op):
            for way in range(2):
                y_copy(op, way, 2, True)[1].wait_recv()

        def cross_send(dy):
            s = dy % SIDE
            there = held[c].at[blk(0, dy)]
            for way in range(2):
                launch(
                    ("F", s),
                    remote(
                        foreign(dy),
                        there,
                        cross_sem.at[0, s, way],
                        cross_sem.at[1, s, way],
                        device((1, -1)[way], 0),
                    ),
                )
            launch(
                key_of(0, dy),
                remote(there, there, cross_sem.at[0, s, 2], cross_sem.at[1, s, 2], device(2, 0)),
            )

        def cross_recv(dy, way):
            s = dy % SIDE
            ref = held[c].at[blk((-1, 1, 2)[way], dy)]
            remote(
                ref, ref, cross_sem.at[0, s, way], cross_sem.at[1, s, way], device(2, 0)
            ).wait_recv()

        done = {}

        def unit(cls, block, ends):
            depth = widths[cls] // 2

            def body(index, carry):
                gate, upper = carry
                low = pl.multiple_of(index * depth, depth)
                deep = pl.ds(pl.multiple_of(offsets[cls] + low, 128), depth)
                piece = held[cls][block, :, pl.ds(low, depth)]
                return (
                    gate + jnp.dot(piece, gate_ref[deep, :], preferred_element_type=F32),
                    upper + jnp.dot(piece, up_ref[deep, :], preferred_element_type=F32),
                )

            if ends:
                start = (total[block, :, 0:units], total[block, :, units : 2 * units])
            else:
                start = (jnp.zeros((rows, units), F32), jnp.zeros((rows, units), F32))
            gate, upper = lax.fori_loop(0, 2, body, start)
            if ends:
                hidden[block] = (jax.nn.silu(gate) * upper).astype(BF)
            else:
                total[block, :, 0:units] = gate
                total[block, :, units : 2 * units] = upper

        def compute(cls, places):
            if cls != c:
                for place in places:
                    chip_copy(cls, *place).wait_recv()
            for ends in (False, True):
                group = [p for p in places if (key_of(*p) in done) == ends]
                if not group:
                    continue

                def body(index, carry):
                    block = blk(*group[0])
                    for number in range(1, len(group)):
                        block = jnp.where(index == number, blk(*group[number]), block)
                    unit(cls, block, ends)
                    return carry

                if len(group) == 1:
                    body(0, 0)
                else:
                    lax.fori_loop(0, len(group), body, 0)
            for place in places:
                done[key_of(*place)] = True

        beside_y = [(0, -1), (0, 1)]
        if c == 0:
            cross_send(0)
            y_start(0)
            share(0, 0)
            loaded(0)
            loaded(1)
            compute(0, [(0, 0)])
            compute(1, [(0, 0)])
            for way in range(2):
                y_full_recv(0, way)
                share(*beside_y[way])
            compute(0, beside_y)
            compute(1, beside_y)
            for way, dx in enumerate((-1, 1, 2)):
                cross_recv(0, way)
                y_start(dx % SIDE)
                share(dx, 0)
            swap_down()
            compute(0, [(-1, 0), (1, 0), (2, 0)])
            y_half_recv(0)
            share(0, 2)
            compute(1, [(-1, 0), (1, 0), (2, 0)])
            compute(0, [(0, 2)])
            compute(1, [(0, 2)])
            for dx in (-1, 1, 2):
                for way in range(2):
                    y_full_recv(dx % SIDE, way)
                    share(dx, (-1, 1)[way])
                compute(0, [(dx, -1), (dx, 1)])
                if dx != 2:
                    compute(1, [(-1, dx), (1, dx), (2, dx)])
            for dx in (-1, 1):
                y_half_recv(dx % SIDE)
                share(dx, 2)
                compute(0, [(dx, 2)])
            y_half_recv(2)
            share(2, 2)
            compute(0, [(2, 2)])
            compute(1, [(-1, 2), (1, 2), (2, 2)])
        else:
            y_start(0)
            y_start(1)
            cross_send(0)
            share(0, 0)
            loaded(0)
            loaded(1)
            compute(1, [(0, 0)])
            compute(0, [(0, 0)])
            for way in range(2):
                for op in range(2):
                    y_full_recv(op, way)
                cross_send((-1, 1)[way])
                share(*beside_y[way])
            compute(1, beside_y)
            compute(0, beside_y)
            for way, dx in enumerate((-1, 1, 2)):
                cross_recv(0, way)
                share(dx, 0)
            compute(1, [(-1, 0), (1, 0), (2, 0)])
            for op in range(2):
                y_half_recv(op)
            cross_send(2)
            swap_down()
            share(0, 2)
            compute(0, [(-1, 0), (1, 0), (2, 0)])
            compute(1, [(0, 2)])
            compute(0, [(0, 2)])
            for dy in (-1, 1):
                for way, dx in enumerate((-1, 1, 2)):
                    cross_recv(dy, way)
                    share(dx, dy)
                compute(1, [(-1, dy), (1, dy), (2, dy)])
                compute(0, [(dy, -1), (dy, 1)])
            compute(0, [(2, -1), (2, 1)])
            compute(0, [(-1, 2), (1, 2)])
            for way, dx in enumerate((-1, 1, 2)):
                cross_recv(2, way)
                share(dx, 2)
            compute(1, [(-1, 2), (1, 2), (2, 2)])
            compute(0, [(2, 2)])

        loaded(2)
        def product(cls, block, dest, terms):
            span = widths[cls] // 2
            step = span // 2
            for part in range(2):

                def body(index, carry):
                    low = pl.multiple_of(index * step, 128)
                    here = pl.multiple_of(low + part * span, 128)
                    columns = pl.ds(here, step)
                    value = None
                    if block is not None:
                        value = jnp.dot(
                            hidden[block],
                            down_ref[:, pl.ds(pl.multiple_of(here + offsets[cls], 128), step)],
                            preferred_element_type=F32,
                        )
                    for get, which in terms:
                        if which is None:
                            term = get(columns).astype(F32)
                        elif which == part:
                            term = get(pl.ds(low, step)).astype(F32)
                        else:
                            continue
                        value = term if value is None else value + term
                    dest[:, columns] = value.astype(BF)
                    return carry

                lax.fori_loop(0, span // step, body, 0)

        orders = (
            [(2, 2), (1, 2), (-1, 2), (0, 2), (2, 1), (2, -1), (1, 1), (1, -1), (2, 0)]
            + [(-1, 1), (-1, -1), (1, 0), (0, 1), (0, -1), (-1, 0), (0, 0)],
            [(2, 2), (1, 2), (-1, 2), (2, 1), (1, 1), (-1, 1), (0, 2), (2, -1), (1, -1)]
            + [(-1, -1), (2, 0), (1, 0), (-1, 0), (0, 1), (0, -1), (0, 0)],
        )
        queue = list(orders[1 - c])

        def inner_copy(cls, dx, dy):
            i = dx % SIDE * SIDE + dy % SIDE
            return remote(
                held[cls].at[blk(dx, dy)],
                inner.at[blk(dx, dy), :, pl.ds(0, widths[cls])],
                r_chip_sem.at[0, i],
                r_chip_sem.at[1, i],
                sibling,
            )

        def feed():
            if queue:
                dx, dy = queue.pop(0)
                block = blk(dx, dy)
                product(1 - c, block, held[1 - c].at[block], ())
                launch(("chip", dx, dy), inner_copy(1 - c, dx, dy))

        served = []

        def chip_sum(dx, dy, terms):
            served.append((dx, dy))
            block = blk(dx, dy)
            inner_copy(c, dx, dy).wait_recv()
            settle(key_of(dx, dy))
            product(
                c,
                block,
                held[c].at[block],
                [(lambda columns: inner[block, :, columns], None)] + terms,
            )
            feed()

        def ring_back(op, way, ref, is_half):
            if is_half:
                return remote(
                    ref.at[:, pl.ds(way * half, half)],
                    r_half.at[op, way, :, pl.ds(0, half)],
                    r_ring_sem.at[0, op, way],
                    r_ring_sem.at[1, op, way],
                    device(0, (1, -1)[way]),
                )
            return remote(
                ref,
                r_full.at[op, way, :, pl.ds(0, width)],
                r_ring_sem.at[0, op, 2 + way],
                r_ring_sem.at[1, op, 2 + way],
                device(0, (1, -1)[way]),
            )

        def half_term(op, way):
            ring_back(op, way, held[c].at[0], True).wait_recv()
            return (lambda columns: r_half[op, way, :, columns], way)

        def full_terms(op):
            for way in range(2):
                ring_back(op, way, held[c].at[0], False).wait_recv()
            return [
                (lambda columns: r_full[op, 0, :, columns], None),
                (lambda columns: r_full[op, 1, :, columns], None),
            ]

        def crossed(s, way):
            return x_recv0.at[way] if c == 0 else x_recv1.at[s, way]

        def cross_back(s, way, ref):
            return remote(
                ref,
                crossed(s, way),
                r_cross_sem.at[0, s, way],
                r_cross_sem.at[1, s, way],
                device((1, -1, 2)[way], 0),
            )

        def cross_term(s, way):
            cross_back(s, way, held[c].at[0]).wait_recv()
            return (lambda columns: crossed(s, way)[:, columns], None)

        ours, theirs = held[c].at[blk(0, 0)], foreign(0)
        feed()
        feed()
        if c == 0:

            def far(dx):
                chip_sum(dx, 2, [])
                for way in range(2):
                    launch("back", ring_back(dx % SIDE, way, held0.at[blk(dx, 2)], True))

            def near(dx):
                for way in range(2):
                    dy = (1, -1)[way]
                    chip_sum(dx, dy, [half_term(dx % SIDE, way)])
                    launch("back", ring_back(dx % SIDE, way, held0.at[blk(dx, dy)], False))

            def home(dx):
                terms = full_terms(dx % SIDE)
                if dx == 0:
                    terms.append(cross_term(0, 2))
                chip_sum(dx, 0, terms)
                if dx != 0:
                    way = {1: 0, -1: 1, 2: 2}[dx]
                    launch("back", cross_back(0, way, held0.at[blk(dx, 0)]))

            for dx in (2, 1, -1, 0):
                far(dx)
            near(2)
            near(1)
            home(2)
            near(-1)
            home(1)
            near(0)
            home(-1)
            home(0)
            settle(("F", 0))
            product(0, None, theirs, [cross_term(0, 0), cross_term(0, 1)])
        else:

            def away(dy):
                for way, dx in ((2, 2), (0, 1), (1, -1)):
                    chip_sum(dx, dy, [])
                    launch("back", cross_back(dy % SIDE, way, held1.at[blk(dx, dy)]))

            def home(dy):
                s = dy % SIDE
                extra = ([], [])
                for op in range(2):
                    if dy in (1, -1):
                        extra[op].append(half_term(op, (1, -1).index(dy)))
                    if dy == 0:
                        extra[op].extend(full_terms(op))
                chip_sum(0, dy, [cross_term(s, 2)] + extra[0])
                settle(("F", s))
                other = foreign(dy)
                product(1, None, other, [cross_term(s, 0), cross_term(s, 1)] + extra[1])
                for op, ref in enumerate((held1.at[blk(0, dy)], other)):
                    if dy == 2:
                        for way in range(2):
                            launch("back", ring_back(op, way, ref, True))
                    elif dy != 0:
                        launch("back", ring_back(op, (1, -1).index(dy), ref, False))

            away(2)
            away(1)
            home(2)
            away(-1)
            away(0)
            home(1)
            home(-1)
            home(0)
        assert served == orders[c] and not queue

        outs = (out0_ref, out1_ref)
        incoming = last.at[:, pl.ds(0, widths[1 - c])]

        def finish(keep, give):
            copy = remote(
                give, last.at[:, pl.ds(0, width)], last_sem.at[0], last_sem.at[1], sibling
            )
            copy.start()
            outs[c][...] = keep[...]
            remote(incoming, incoming, last_sem.at[0], last_sem.at[1], sibling).wait_recv()
            copy.wait_send()

        @pl.when(kind == c)
        def _():
            finish(ours, theirs)

        @pl.when(kind != c)
        def _():
            finish(theirs, ours)

        outs[1 - c][...] = incoming[...]
        for key in list(pending):
            settle(key)

    for c in range(2):
        pl.when(core == c)(functools.partial(run, c))


def on_device(n_node, n_local):
    def run(
        patches,
        norm_gain,
        vit_up,
        vit_down,
        adapter,
        text_rows,
        router,
        expert_ids,
        w_gate,
        w_up,
        w_down,
    ):
        vmem = pl.BlockSpec(memory_space=pltpu.VMEM)
        hbm = pl.BlockSpec(memory_space=pl.ANY)
        row_count, model = expert_ids.shape[0], adapter.shape[1]
        experts = router.shape[1]
        capacity = 7 * row_count // (8 * n_node)
        rows, width = patches.shape
        lanes = 128 * ((width // n_local + 127) // 128)
        own_rows = n_node * capacity
        units = w_gate.shape[2]
        half = model // 2
        first = model * 3 // 5 // 512 * 512
        second = model - first
        swapped = [jax.ShapeDtypeStruct(w.shape[1:], BF) for w in (w_gate, w_up)]
        own, gate_swap, up_swap = pl.pallas_call(
            functools.partial(vision_kernel, n_node, n_local, capacity, first),
            out_shape=[jax.ShapeDtypeStruct((2, own_rows, first), BF)] + swapped,
            in_specs=[hbm, vmem, hbm, hbm, hbm, hbm, vmem, vmem] + [hbm] * 2,
            out_specs=[vmem] + [hbm] * 2,
            scratch_shapes=[
                pltpu.VMEM(patches.shape, BF),
                pltpu.VMEM(vit_up.shape[::-1], BF),
                pltpu.VMEM(vit_down.shape, BF),
                pltpu.VMEM(adapter.shape, BF),
                pltpu.VMEM(text_rows.shape, BF),
                pltpu.SemaphoreType.DMA((5,)),
                pltpu.VMEM((2, experts, PAD, first + row_count), BF),
                pltpu.VMEM((n_node, 2, PAD, first + row_count), BF),
                pltpu.VMEM((2, PAD, first // 2), BF),
                pltpu.VMEM((n_node, PAD, first // 2), BF),
                pltpu.VMEM((n_local, rows, lanes), BF),
                pltpu.VMEM((n_local, rows, lanes), BF),
                pltpu.VMEM((n_local, rows, lanes), BF),
                pltpu.VMEM((n_local, 2 * rows // n_local, half), BF),
                pltpu.VMEM((SIDE, SIDE, 2 * rows // n_local, half), BF),
                pltpu.VMEM((SIDE, 2 * rows // n_local, half), BF),
                pltpu.VMEM((SIDE, 2 * rows // n_local, half), BF),
                pltpu.SemaphoreType.DMA((4, n_local)),
                pltpu.SemaphoreType.DMA((4, n_node)),
                pltpu.SemaphoreType.DMA((2, 2, 8)),
            ],
            compiler_params=pltpu.CompilerParams(
                collective_id=0,
                has_side_effects=True,
                vmem_limit_bytes=63_400_000,
            ),
        )(
            patches,
            norm_gain,
            vit_up.T,
            vit_down,
            adapter,
            text_rows,
            router.T,
            expert_ids.reshape(1, -1),
            w_gate,
            w_up,
        )
        result = pl.pallas_call(
            expert_kernel,
            out_shape=[jax.ShapeDtypeStruct((own_rows, size), BF) for size in (first, second)],
            in_specs=[hbm] * 6,
            out_specs=[vmem] * 2,
            scratch_shapes=[
                pltpu.VMEM((model, units), BF),
                pltpu.VMEM((model, units), BF),
                pltpu.VMEM((units, model), BF),
                pltpu.VMEM((n_local, own_rows, first), BF),
                pltpu.VMEM((n_local, own_rows, second), BF),
                pltpu.VMEM((own_rows, first), BF),
                pltpu.VMEM((SIDE, own_rows, second), BF),
                pltpu.VMEM((n_local, own_rows, 2 * units), F32),
                pltpu.VMEM((n_local, own_rows, units), BF),
                pltpu.VMEM((n_local, own_rows, first), BF),
                pltpu.VMEM((SIDE, 2, own_rows, first // 2), BF),
                pltpu.VMEM((SIDE, 2, own_rows, first), BF),
                pltpu.VMEM((3, own_rows, first), BF),
                pltpu.VMEM((SIDE, 3, own_rows, second), BF),
                pltpu.VMEM((own_rows, first), BF),
                pltpu.SemaphoreType.DMA((5,)),
                pltpu.SemaphoreType.DMA((2, 2)),
                pltpu.SemaphoreType.DMA((2, SIDE, 4)),
                pltpu.SemaphoreType.DMA((2, SIDE, 3)),
                pltpu.SemaphoreType.DMA((2, n_local)),
                pltpu.SemaphoreType.DMA((2, SIDE, 4)),
                pltpu.SemaphoreType.DMA((2, SIDE, 3)),
                pltpu.SemaphoreType.DMA((2, n_local)),
                pltpu.SemaphoreType.DMA((2,)),
            ],
            compiler_params=pltpu.CompilerParams(
                collective_id=1,
                has_side_effects=True,
                vmem_limit_bytes=63_400_000,
            ),
        )(own, w_gate, w_up, w_down, gate_swap, up_swap)
        return jnp.concatenate(result, axis=1)[None]

    return run


def solution(mesh):
    in_specs = (
        P("node", None),
        P(),
        P(None, "local"),
        P("local", None),
        P("local", None),
        P(("node", "local"), None),
        P(),
        P(("node", "local"), None),
        P("node", None, "local"),
        P("node", None, "local"),
        P("node", "local", None),
    )
    out_specs = P("node", "local", None)
    return jax.shard_map(
        on_device(mesh.shape["node"], mesh.shape["local"]),
        mesh=mesh,
        in_specs=in_specs,
        out_specs=out_specs,
        check_vma=False,
    )
```
